512 devices in a mesh: group: 16 (over x, y_hi, core), sub: 32 (over y_lo, z).
Axes of the slice: x: 4, y: 8 (y_hi: 2, y_lo: 4; y = y_hi * 4 + y_lo), z: 8, core: 2. Of those that a mesh axis runs over, the one named last changes fastest.
Arguments:
- fine_residual: bfloat16 [2, 12, 4, 524288], P(None, None, None, ('group', 'sub')), may hold values from -6 to 6
- null_vectors: bfloat16 [2, 12, 32, 524288], P(None, None, None, ('group', 'sub')), may hold values from -0.15625 to 0.15625
- agg_map: int32 [512, 1024], P(('group', 'sub')), may hold values from 0 to 1023, each once within a row
- block_owner: int32 [16], replicated, may hold values from 0 to 15, each once
- coarse_links: bfloat16 [9, 16, 32, 2, 2, 64, 64], P(None, 'group', 'sub'), may hold values from -0.125 to 0.125
Outputs:
- coarse_solution: float32 [16, 32, 2, 2, 4, 64], P('group', 'sub')
- correction: bfloat16 [2, 12, 4, 524288], P(None, None, None, ('group', 'sub'))
The draws below stay inside these ranges and needn't reach their ends.
Inputs may be any that keep to these rules, and one draw needn't show every extreme that they name: `agg_map`: each row lists every local fine site of its device exactly once. `block_owner`: each group holds a different coarse block.
All inputs are finite; a program needn't handle non-finite values.
Results may differ from the reference program's by a relative error of at most 0.015.
Values may be sent and summed in bfloat16 or wider, within the bound.
A program may use at most 64 MiB of HBM per device.

```python
import jax
import jax.numpy as jnp
from jax import lax

SPIN_COLOR = 12
NULLV = 32
AGG = 256
COARSE_STEPS = 4
RHS = 4
BT = 1
CY = 2
CZ = 2
CDOF = 64
FS = 1024
NXC = 16
NTC = 32
N_GROUP = 16
N_SUB = 32
DEVICES = 512


def block_scale(rng, shape, cuts, low, high):
    loudness = 1.0
    for axis_at, shards_of in cuts:
        steps = jax.random.uniform(jax.random.fold_in(jax.random.fold_in(rng, 6), axis_at), (shards_of,), jnp.float32, low / len(cuts), high / len(cuts))
        loudness = loudness * jnp.repeat(jnp.exp(steps), shape[axis_at] // shards_of).reshape((-1,) + (1,) * (len(shape) - 1 - axis_at))
    return loudness


def gaussian(rng, extent, scale, reach, pieces=(), dtype=jnp.bfloat16):
    result = jax.random.normal(rng, extent, jnp.float32) * scale
    if len(pieces) > 0:
        result = block_scale(rng, extent, pieces, -0.22, 0.18) * result
    return jnp.clip(result, min=-reach, max=reach).astype(dtype)


def setup_inputs(seed: int = 0) -> dict:
    key_list = jax.random.split(jax.random.key(seed), 6)
    return {
        "fine_residual": gaussian(key_list[0], (2, SPIN_COLOR, RHS, DEVICES * FS), 1.0, 6.0, ((3, 512),)),
        "null_vectors": gaussian(key_list[1], (2, SPIN_COLOR, NULLV, DEVICES * FS), (2 * (2 * SPIN_COLOR * AGG) ** -0.5), 0.15625, ((3, 512),)),
        "agg_map": jax.vmap(lambda own: jax.random.permutation(own, FS))(jax.random.split(key_list[2], DEVICES)).reshape((DEVICES, FS)).astype(jnp.int32),
        "block_owner": jax.random.permutation(key_list[3], N_GROUP).astype(jnp.int32),
        "coarse_links": gaussian(key_list[4], (9, NXC, NTC, CY, CZ, CDOF, CDOF), (36 * CDOF) ** -0.5, 0.125, ((1, 16), (2, 32))),
    }


HIGHEST = lax.Precision.HIGHEST


def neighbour(field, stride, axis_number):
    length = field.shape[axis_number]
    widths = [(0, 0)] * field.ndim
    widths[axis_number] = (1, 1)
    padded = jnp.pad(field, widths)
    return lax.slice_in_dim(padded, 1 + stride, 1 + stride + length, axis=axis_number)


def hopping(coarse_links, field):
    summed = jnp.einsum('xtyzij,xtyzrj->xtyzri', coarse_links[0].astype(jnp.float32), field, precision=HIGHEST)
    direction = 1
    for axis_number in range(4):
        for stride in (1, -1):
            if axis_number < 2:
                shifted = jnp.roll(field, -stride, axis=axis_number)
            else:
                shifted = neighbour(field, stride, axis_number)
            summed = summed + jnp.einsum('xtyzij,xtyzrj->xtyzri', coarse_links[direction].astype(jnp.float32), shifted, precision=HIGHEST)
            direction = direction + 1
    return summed


def reference(fine_residual, null_vectors, agg_map, block_owner, coarse_links):
    ndevices = agg_map.shape[0]
    naggs = BT * CY * CZ
    fine_dev = fine_residual.astype(jnp.float32).reshape(2, SPIN_COLOR, RHS, ndevices, FS)
    null_dev = null_vectors.astype(jnp.float32).reshape(2, SPIN_COLOR, NULLV, ndevices, FS)
    fine_agg = jnp.take_along_axis(fine_dev, jnp.broadcast_to(agg_map[None, None, None], fine_dev.shape), axis=4)
    null_agg = jnp.take_along_axis(null_dev, jnp.broadcast_to(agg_map[None, None, None], null_dev.shape), axis=4)
    fine_agg = fine_agg.reshape(2, SPIN_COLOR, RHS, ndevices, naggs, AGG)
    null_agg = null_agg.reshape(2, SPIN_COLOR, NULLV, ndevices, naggs, AGG)
    form = 'fcdas,frdas->darc'
    real_part = jnp.einsum(form, null_agg[0], fine_agg[0], precision=HIGHEST) + jnp.einsum(form, null_agg[1], fine_agg[1], precision=HIGHEST)
    imag_part = jnp.einsum(form, null_agg[0], fine_agg[1], precision=HIGHEST) - jnp.einsum(form, null_agg[1], fine_agg[0], precision=HIGHEST)
    per_device = jnp.concatenate([real_part, imag_part], axis=-1)
    per_device = per_device.reshape(N_GROUP, N_SUB * BT, CY, CZ, RHS, CDOF)
    coarse_rhs = jnp.zeros_like(per_device).at[block_owner].set(per_device)
    iterate = coarse_rhs
    for step in range(COARSE_STEPS):
        low = lax.optimization_barrier(iterate.astype(jnp.bfloat16)).astype(jnp.float32)
        iterate = coarse_rhs - hopping(coarse_links, low)
    rounded = lax.optimization_barrier(iterate.astype(jnp.bfloat16)).astype(jnp.float32)
    own_blocks = rounded[block_owner].reshape(ndevices, naggs, RHS, CDOF)
    part_re = own_blocks[..., :NULLV]
    part_im = own_blocks[..., NULLV:]
    back = 'fcdas,darc->frdas'
    corr_re = jnp.einsum(back, null_agg[0], part_re, precision=HIGHEST) - jnp.einsum(back, null_agg[1], part_im, precision=HIGHEST)
    corr_im = jnp.einsum(back, null_agg[0], part_im, precision=HIGHEST) + jnp.einsum(back, null_agg[1], part_re, precision=HIGHEST)
    stacked = jnp.stack([corr_re, corr_im]).reshape(2, SPIN_COLOR, RHS, ndevices, FS)
    inverse_map = jnp.argsort(agg_map, axis=1).astype(jnp.int32)
    ordered = jnp.take_along_axis(stacked, jnp.broadcast_to(inverse_map[None, None, None], stacked.shape), axis=4)
    correction = ordered.reshape(2, SPIN_COLOR, RHS, ndevices * FS).astype(jnp.bfloat16)
    return iterate, correction
```

```python
import functools

import jax
import jax.numpy as jnp
from jax import lax
from jax.experimental import pallas as pl
from jax.experimental.pallas import tpu as pltpu
from jax.sharding import PartitionSpec as P

SPIN_COLOR = 12
NULLV = 32
AGG = 256
COARSE_STEPS = 4
RHS = 4
CDOF = 64
NAGG = 4
FS = NAGG * AGG
FBLOCK = 4
NBLOCK = SPIN_COLOR // FBLOCK
MESH = pl.DeviceIdType.MESH
F32 = jnp.float32
BF16 = jnp.bfloat16


def site_masks(agg_row):
    high = agg_row // 128
    low = agg_row % 128
    lanes = lax.broadcasted_iota(jnp.int32, (128, FS), 0)
    low_hot = jnp.where(lanes == low, 1.0, 0.0).astype(BF16)
    row = lax.broadcasted_iota(jnp.int32, (32, FS), 0)
    place = lax.broadcasted_iota(jnp.int32, (32, FS), 1)
    high_hot = jnp.where((row % 8 == high) & (row // 8 == place // AGG), 1.0, 0.0).astype(BF16)
    grid = lax.dot_general(
        high_hot, low_hot, (((1,), (1,)), ((), ())), preferred_element_type=F32
    )
    return [
        jnp.concatenate([grid[a * 8 + h : a * 8 + h + 1] for h in range(8)], axis=1)
        for a in range(NAGG)
    ]


def fold_lanes(tile):
    tile = tile + pltpu.roll(tile, 64, 1)
    return tile + pltpu.roll(tile, 32, 1)


def restricted_piece(total, row, lane):
    per_agg = []
    for a in range(NAGG):
        parts = []
        for ri in range(2):
            kept = jnp.zeros((8, 128), F32)
            for f in range(FBLOCK):
                at = (f * NAGG + a) * 8
                tile = total[at : at + 8, ri * 128 : (ri + 1) * 128]
                kept = kept + jnp.where(lane // NULLV == f, tile, 0.0)
            parts.append(fold_lanes(kept))
        by_re, by_im = parts
        real = by_re + pltpu.roll(by_im, 4, 0)
        imag = pltpu.roll(by_re, 4, 0) - by_im
        per_agg.append(jnp.where((lane // NULLV) % 2 == 0, real, imag))
    upper = jnp.where(lane < CDOF, per_agg[0], per_agg[1])
    lower = jnp.where(lane < CDOF, per_agg[2], per_agg[3])
    return jnp.where(row < 4, upper, pltpu.roll(lower, 4, 0))


def prolongation_rows(piece, row, lane):
    block = lane // NULLV
    swapped = pltpu.roll(piece, 4, 0)
    doubled = (jnp.where(row < 4, piece, swapped), jnp.where(row < 4, swapped, piece))
    rows = []
    for y in range(2):
        for z in range(2):
            re, im = (
                fold_lanes(jnp.where(block == 2 * z + part, doubled[y], 0.0)) for part in range(2)
            )
            for left, right in ((re, -im), (im, re)):
                for pair in range(2):
                    same = block == 2 * pair + row // RHS
                    rows.append(
                        jnp.concatenate(
                            [jnp.where(same, left, 0.0), jnp.where(same, right, 0.0)], axis=1
                        )
                    )
    return jnp.concatenate(rows, axis=0).astype(BF16)


def build_operator(links, weights):
    zero = jnp.zeros((CDOF, CDOF), BF16)

    def sited(block, z):
        return jnp.concatenate([block, zero] if z == 0 else [zero, block], axis=1)

    for y in range(2):
        for z in range(2):
            n = 2 * y + z
            here = links[0 * 4 + n]
            across = links[(7 + z) * 4 + n]
            columns = [
                jnp.concatenate([here, across] if z == 0 else [across, here], axis=1),
                sited(links[(5 + y) * 4 + n], z),
            ] + [sited(links[k * 4 + n], z) for k in (1, 2, 3, 4)]
            for source, column in enumerate(columns):
                weights[source * 128 : (source + 1) * 128, n * CDOF : (n + 1) * CDOF] = column.T


def hop(weights, here, others, row):
    low = [here, pltpu.roll(here, 4, 0)] + list(others)
    low = jnp.concatenate(low, axis=1).astype(BF16)
    out = jnp.dot(low, weights[...], preferred_element_type=F32)
    return jnp.where(row < 4, out[:, :128], out[:, 128:])


def kernel(
    n_group,
    n_sub,
    owner_ref,
    fine_ref,
    null_ref,
    agg_ref,
    links_ref,
    sol_ref,
    corr_ref,
    fine,
    null,
    agg,
    links,
    weights,
    rhs_out,
    rhs_in,
    iter_out,
    iter_in,
    last_out,
    last_in,
    local_sem,
    rhs_send,
    rhs_recv,
    iter_send,
    iter_recv,
    last_send,
    last_recv,
):
    g = lax.axis_index("group")
    s = lax.axis_index("sub")

    def device(dg, ds):
        return lax.rem(g + dg, n_group), lax.rem(s + ds, n_sub)

    load_agg = pltpu.make_async_copy(agg_ref, agg, local_sem.at[0])
    load_fine = pltpu.make_async_copy(fine_ref, fine, local_sem.at[1])
    load_links = pltpu.make_async_copy(links_ref, links, local_sem.at[2])
    load_null = [
        pltpu.make_async_copy(
            null_ref.at[:, pl.ds(b * FBLOCK, FBLOCK)],
            null.at[:, pl.ds(b * FBLOCK, FBLOCK)],
            local_sem.at[3 + b],
        )
        for b in range(NBLOCK)
    ]
    load_agg.start()
    load_fine.start()
    for load in load_null:
        load.start()
    load_links.start()

    barrier = pltpu.get_barrier_semaphore()
    n_far = 3 * n_group - 1

    def offsets(i):
        at = i // n_group
        return lax.rem(i, n_group), lax.rem(at * (n_sub - 1) + (at // 2) * 3, n_sub)

    def greet(i, carry):
        pl.semaphore_signal(barrier, inc=1, device_id=device(*offsets(i)), device_id_type=MESH)
        return carry

    lax.fori_loop(1, n_far + 1, greet, 0)

    row = lax.broadcasted_iota(jnp.int32, (8, 128), 0)
    lane = lax.broadcasted_iota(jnp.int32, (8, 128), 1)

    load_agg.wait()
    masks = site_masks(agg[...])
    load_fine.wait()
    total = jnp.zeros((128, 256), F32)
    for b in range(NBLOCK):
        spread = []
        for f in range(b * FBLOCK, (b + 1) * FBLOCK):
            psi = jnp.concatenate([fine[0, f].astype(F32), fine[1, f].astype(F32)], axis=0)
            spread += [psi * masks[a] for a in range(NAGG)]
        spread = jnp.concatenate(spread, axis=0).astype(BF16)
        load_null[b].wait()
        part = null[:, b * FBLOCK : (b + 1) * FBLOCK].reshape(2 * FBLOCK * NULLV, FS)
        total = total + lax.dot_general(
            spread, part, (((1,), (1,)), ((), ())), preferred_element_type=F32
        )
    mine = restricted_piece(total, row, lane).astype(BF16)
    rhs_out[...] = mine
    rhs_in[0, g] = mine

    pl.semaphore_wait(barrier, n_far)

    def rhs_copy(i):
        dg, ds = offsets(i)
        at = i // n_group
        return pltpu.make_async_remote_copy(
            src_ref=rhs_out,
            dst_ref=rhs_in.at[at, g],
            send_sem=rhs_send.at[i],
            recv_sem=rhs_recv.at[at, g],
            device_id=device(dg, ds),
            device_id_type=MESH,
        )

    def rhs_start(i, carry):
        rhs_copy(i).start()
        return carry

    lax.fori_loop(1, n_far + 1, rhs_start, 0)

    load_links.wait()
    build_operator(links, weights)

    def rhs_wait(i, carry):
        at = i // n_group
        source = lax.rem(g + i, n_group)
        pltpu.make_async_remote_copy(
            src_ref=rhs_out,
            dst_ref=rhs_in.at[at, source],
            send_sem=rhs_send.at[i],
            recv_sem=rhs_recv.at[at, source],
            device_id=device(0, 1),
            device_id_type=MESH,
        ).wait_recv()
        return carry

    lax.fori_loop(1, n_far + 1, rhs_wait, 0)

    def chosen(at, x):
        picked = jnp.zeros((8, 128), F32)
        for k in range(n_group):
            picked = picked + jnp.where(owner_ref[k] == x, rhs_in[at, k].astype(F32), 0.0)
        return picked

    ahead_x = lax.rem(g + 1, n_group)
    behind_x = lax.rem(g + n_group - 1, n_group)
    rhs = chosen(0, g)
    others = [chosen(0, ahead_x), chosen(0, behind_x), chosen(1, g), chosen(2, g)]
    iterate = rhs - hop(weights, rhs, others, row)

    steps = [(n_group - 1, 0), (1, 0), (0, n_sub - 1), (0, 1)]
    pending = []
    for step in range(COARSE_STEPS - 1):
        iter_out[step] = iterate
        copies = [
            pltpu.make_async_remote_copy(
                src_ref=iter_out.at[step],
                dst_ref=iter_in.at[step, way],
                send_sem=iter_send.at[step, way],
                recv_sem=iter_recv.at[step, way],
                device_id=device(*steps[way]),
                device_id_type=MESH,
            )
            for way in range(4)
        ]
        for copy in copies:
            copy.start()
        for copy in copies:
            copy.wait_recv()
        pending += copies
        iterate = rhs - hop(weights, iterate, [iter_in[step, way] for way in range(4)], row)

    rounded = iterate.astype(BF16)
    last_out[...] = rounded
    last_in[g] = rounded

    def last_copy(i, at):
        return pltpu.make_async_remote_copy(
            src_ref=last_out,
            dst_ref=last_in.at[at],
            send_sem=last_send.at[i],
            recv_sem=last_recv.at[at],
            device_id=device(i, 0),
            device_id_type=MESH,
        )

    def last_start(i, carry):
        last_copy(i, g).start()
        return carry

    lax.fori_loop(1, n_group, last_start, 0)
    for y in range(2):
        for z in range(2):
            sol_ref[y, z] = iterate[y * RHS : (y + 1) * RHS, z * CDOF : (z + 1) * CDOF]

    def last_wait(i, carry):
        last_copy(i, lax.rem(g + i, n_group)).wait_recv()
        return carry

    lax.fori_loop(1, n_group, last_wait, 0)

    block_here = jnp.int32(0)
    for k in range(n_group):
        block_here = block_here + jnp.where(g == k, owner_ref[k], 0)
    own = jnp.zeros((8, 128), F32)
    for k in range(n_group):
        own = own + jnp.where(block_here == k, last_in[k].astype(F32), 0.0)

    left = prolongation_rows(own, row, lane)
    for b in range(NBLOCK):
        part = null[:, b * FBLOCK : (b + 1) * FBLOCK].reshape(2 * FBLOCK * NULLV, FS)
        wide = jnp.dot(left, part, preferred_element_type=F32)
        here = wide[:32] * masks[0]
        for a in range(1, NAGG):
            here = here + wide[a * 32 : (a + 1) * 32] * masks[a]
        for ri in range(2):
            for f in range(FBLOCK):
                at = (ri * FBLOCK + f) * RHS
                corr_ref[ri, b * FBLOCK + f] = here[at : at + RHS].astype(BF16)

    def rhs_done(i, carry):
        rhs_copy(i).wait_send()
        return carry

    lax.fori_loop(1, n_far + 1, rhs_done, 0)
    for copy in pending:
        copy.wait_send()

    def last_done(i, carry):
        last_copy(i, g).wait_send()
        return carry

    lax.fori_loop(1, n_group, last_done, 0)


def on_device(n_group, n_sub, fine_residual, null_vectors, agg_map, block_owner, coarse_links):
    any_space = pl.BlockSpec(memory_space=pl.ANY)
    vmem = pl.BlockSpec(memory_space=pltpu.VMEM)
    dma = pltpu.SemaphoreType.DMA
    exchanges = COARSE_STEPS - 1
    solution_here, correction = pl.pallas_call(
        functools.partial(kernel, n_group, n_sub),
        out_shape=(
            jax.ShapeDtypeStruct((2, 2, RHS, CDOF), F32),
            jax.ShapeDtypeStruct((2, SPIN_COLOR, RHS, FS), BF16),
        ),
        in_specs=[pl.BlockSpec(memory_space=pltpu.SMEM)] + [any_space] * 4,
        out_specs=(vmem, vmem),
        scratch_shapes=[
            pltpu.VMEM((2, SPIN_COLOR, RHS, FS), BF16),
            pltpu.VMEM((2, SPIN_COLOR, NULLV, FS), BF16),
            pltpu.VMEM((1, FS), jnp.int32),
            pltpu.VMEM((36, CDOF, CDOF), BF16),
            pltpu.VMEM((6 * 128, 256), BF16),
            pltpu.VMEM((8, 128), BF16),
            pltpu.VMEM((3, n_group, 8, 128), BF16),
            pltpu.VMEM((exchanges, 8, 128), F32),
            pltpu.VMEM((exchanges, 4, 8, 128), F32),
            pltpu.VMEM((8, 128), BF16),
            pltpu.VMEM((n_group, 8, 128), BF16),
            dma((3 + NBLOCK,)),
            dma((3 * n_group,)),
            dma((3, n_group)),
            dma((exchanges, 4)),
            dma((exchanges, 4)),
            dma((n_group,)),
            dma((n_group,)),
        ],
        compiler_params=pltpu.CompilerParams(
            collective_id=0, has_side_effects=True, vmem_limit_bytes=32 * 1024 * 1024
        ),
    )(
        block_owner,
        fine_residual,
        null_vectors,
        agg_map,
        coarse_links.reshape(36, CDOF, CDOF),
    )
    return solution_here.reshape(1, 1, 2, 2, RHS, CDOF), correction


def solution(mesh):
    in_specs = (
        P(None, None, None, ("group", "sub")),
        P(None, None, None, ("group", "sub")),
        P(("group", "sub"), None),
        P(),
        P(None, "group", "sub", None, None, None, None),
    )
    out_specs = (P("group", "sub", None, None, None, None), P(None, None, None, ("group", "sub")))
    return jax.shard_map(
        functools.partial(on_device, mesh.shape["group"], mesh.shape["sub"]),
        mesh=mesh,
        in_specs=in_specs,
        out_specs=out_specs,
        check_vma=False,
    )
```

```python
import functools

import jax
import jax.numpy as jnp
from jax import lax
from jax.experimental import pallas as pl
from jax.experimental.pallas import tpu as pltpu
from jax.sharding import PartitionSpec as P

SPIN_COLOR = 12
NULLV = 32
AGG = 256
COARSE_STEPS = 4
RHS = 4
CDOF = 64
NAGG = 4
FS = NAGG * AGG
FBLOCK = 4
NBLOCK = SPIN_COLOR // FBLOCK
MESH = pl.DeviceIdType.MESH
F32 = jnp.float32
BF16 = jnp.bfloat16


def site_masks(agg_row):
    high = agg_row // 128
    low = agg_row % 128
    lanes = lax.broadcasted_iota(jnp.int32, (128, FS), 0)
    low_hot = jnp.where(lanes == low, 1.0, 0.0).astype(BF16)
    row = lax.broadcasted_iota(jnp.int32, (32, FS), 0)
    place = lax.broadcasted_iota(jnp.int32, (32, FS), 1)
    high_hot = jnp.where((row % 8 == high) & (row // 8 == place // AGG), 1.0, 0.0).astype(BF16)
    grid = lax.dot_general(
        high_hot, low_hot, (((1,), (1,)), ((), ())), preferred_element_type=F32
    )
    return [
        jnp.concatenate([grid[a * 8 + h : a * 8 + h + 1] for h in range(8)], axis=1)
        for a in range(NAGG)
    ]


def fold_lanes(tile):
    tile = tile + pltpu.roll(tile, 64, 1)
    return tile + pltpu.roll(tile, 32, 1)


def restricted_piece(total, row, lane):
    per_agg = []
    for a in range(NAGG):
        parts = []
        for ri in range(2):
            kept = jnp.zeros((8, 128), F32)
            for f in range(FBLOCK):
                at = (f * NAGG + a) * 8
                tile = total[at : at + 8, ri * 128 : (ri + 1) * 128]
                kept = kept + jnp.where(lane // NULLV == f, tile, 0.0)
            parts.append(fold_lanes(kept))
        by_re, by_im = parts
        real = by_re + pltpu.roll(by_im, 4, 0)
        imag = pltpu.roll(by_re, 4, 0) - by_im
        per_agg.append(jnp.where((lane // NULLV) % 2 == 0, real, imag))
    upper = jnp.where(lane < CDOF, per_agg[0], per_agg[1])
    lower = jnp.where(lane < CDOF, per_agg[2], per_agg[3])
    return jnp.where(row < 4, upper, pltpu.roll(lower, 4, 0))


def restrict(fine, null, masks, row, lane, loads=()):
    total = jnp.zeros((128, 256), F32)
    for b in range(NBLOCK):
        spread = []
        for f in range(b * FBLOCK, (b + 1) * FBLOCK):
            psi = jnp.concatenate([fine[0, f].astype(F32), fine[1, f].astype(F32)], axis=0)
            spread += [psi * masks[a] for a in range(NAGG)]
        spread = jnp.concatenate(spread, axis=0).astype(BF16)
        for load in loads[b : b + 1]:
            load.wait()
        part = null[:, b * FBLOCK : (b + 1) * FBLOCK].reshape(2 * FBLOCK * NULLV, FS)
        total = total + lax.dot_general(
            spread, part, (((1,), (1,)), ((), ())), preferred_element_type=F32
        )
    return restricted_piece(total, row, lane)


def prolongation_rows(piece, row, lane):
    block = lane // NULLV
    swapped = pltpu.roll(piece, 4, 0)
    doubled = (jnp.where(row < 4, piece, swapped), jnp.where(row < 4, swapped, piece))
    rows = []
    for y in range(2):
        for z in range(2):
            re, im = (
                fold_lanes(jnp.where(block == 2 * z + part, doubled[y], 0.0)) for part in range(2)
            )
            for left, right in ((re, -im), (im, re)):
                for pair in range(2):
                    same = block == 2 * pair + row // RHS
                    rows.append(
                        jnp.concatenate(
                            [jnp.where(same, left, 0.0), jnp.where(same, right, 0.0)], axis=1
                        )
                    )
    return jnp.concatenate(rows, axis=0).astype(BF16)


def prolong_kernel(sol_ref, own_ref, masks_ref, null, sol_out, corr_out, sol, corr, sem):
    row = lax.broadcasted_iota(jnp.int32, (8, 128), 0)
    lane = lax.broadcasted_iota(jnp.int32, (8, 128), 1)
    for y in range(2):
        for z in range(2):
            sol[y, z] = sol_ref[y * RHS : (y + 1) * RHS, z * CDOF : (z + 1) * CDOF]
    stores = [pltpu.make_async_copy(sol, sol_out, sem.at[NBLOCK])]
    stores[0].start()
    left = prolongation_rows(own_ref[...], row, lane)
    for b in range(NBLOCK):
        at_f = pl.ds(b * FBLOCK, FBLOCK)
        part = null[:, b * FBLOCK : (b + 1) * FBLOCK].reshape(2 * FBLOCK * NULLV, FS)
        wide = jnp.dot(left, part, preferred_element_type=F32)
        here = wide[:32] * masks_ref[0:1]
        for a in range(1, NAGG):
            here = here + wide[a * 32 : (a + 1) * 32] * masks_ref[a : a + 1]
        for ri in range(2):
            for f in range(FBLOCK):
                at = (ri * FBLOCK + f) * RHS
                corr[ri, b * FBLOCK + f] = here[at : at + RHS].astype(BF16)
        stores.append(
            pltpu.make_async_copy(corr.at[:, at_f], corr_out.at[:, at_f], sem.at[b])
        )
        stores[-1].start()
    for store in stores:
        store.wait()


def build_operator(links, weights):
    zero = jnp.zeros((CDOF, CDOF), BF16)

    def sited(block, z):
        return jnp.concatenate([block, zero] if z == 0 else [zero, block], axis=1)

    for y in range(2):
        for z in range(2):
            n = 2 * y + z
            here = links[0 * 4 + n]
            across = links[(7 + z) * 4 + n]
            columns = [
                jnp.concatenate([here, across] if z == 0 else [across, here], axis=1),
                sited(links[(5 + y) * 4 + n], z),
            ] + [sited(links[k * 4 + n], z) for k in (1, 2, 3, 4)]
            for source, column in enumerate(columns):
                weights[source * 128 : (source + 1) * 128, n * CDOF : (n + 1) * CDOF] = column.T


def hop(weights, here, others, row):
    low = [here, pltpu.roll(here, 4, 0)] + list(others)
    low = jnp.concatenate(low, axis=1).astype(BF16)
    out = jnp.dot(low, weights[...], preferred_element_type=F32)
    return jnp.where(row < 4, out[:, :128], out[:, 128:])


def kernel(
    n_group,
    n_sub,
    owner_ref,
    fine_ref,
    null_ref,
    agg_ref,
    links_ref,
    sol_ref,
    own_ref,
    masks_ref,
    null,
    fine,
    agg,
    links,
    owner,
    weights,
    rhs_out,
    rhs_in,
    iter_out,
    iter_in,
    last_out,
    last_in,
    local_sem,
    rhs_send,
    rhs_recv,
    iter_send,
    iter_recv,
    last_send,
    last_recv,
):
    g = lax.axis_index("group")
    s = lax.axis_index("sub")

    def device(dg, ds):
        return lax.rem(g + dg, n_group), lax.rem(s + ds, n_sub)

    load_agg = pltpu.make_async_copy(agg_ref, agg, local_sem.at[0])
    load_fine = pltpu.make_async_copy(fine_ref, fine, local_sem.at[1])
    load_links = pltpu.make_async_copy(links_ref, links, local_sem.at[2])
    load_null = [
        pltpu.make_async_copy(
            null_ref.at[:, pl.ds(b * FBLOCK, FBLOCK)],
            null.at[:, pl.ds(b * FBLOCK, FBLOCK)],
            local_sem.at[3 + b],
        )
        for b in range(NBLOCK)
    ]
    load_owner = pltpu.make_async_copy(owner_ref, owner, local_sem.at[3 + NBLOCK])
    load_agg.start()
    load_fine.start()
    for load in load_null:
        load.start()
    load_links.start()
    load_owner.start()

    barrier = pltpu.get_barrier_semaphore()
    n_far = 3 * n_group - 1

    def offsets(i):
        at = i // n_group
        return lax.rem(i, n_group), lax.rem(at * (n_sub - 1) + (at // 2) * 3, n_sub)

    def greet(i, carry):
        pl.semaphore_signal(barrier, inc=1, device_id=device(*offsets(i)), device_id_type=MESH)
        return carry

    lax.fori_loop(1, n_far + 1, greet, 0)

    row = lax.broadcasted_iota(jnp.int32, (8, 128), 0)
    lane = lax.broadcasted_iota(jnp.int32, (8, 128), 1)

    load_agg.wait()
    masks = site_masks(agg[...])
    for a in range(NAGG):
        masks_ref[a : a + 1] = masks[a]
    load_fine.wait()
    mine = restrict(fine, null, masks, row, lane, load_null).astype(BF16)
    rhs_out[...] = mine
    rhs_in[0, g] = mine

    pl.semaphore_wait(barrier, n_far)

    def rhs_copy(i):
        dg, ds = offsets(i)
        at = i // n_group
        return pltpu.make_async_remote_copy(
            src_ref=rhs_out,
            dst_ref=rhs_in.at[at, g],
            send_sem=rhs_send.at[i],
            recv_sem=rhs_recv.at[at, g],
            device_id=device(dg, ds),
            device_id_type=MESH,
        )

    def rhs_start(i, carry):
        rhs_copy(i).start()
        return carry

    lax.fori_loop(1, n_far + 1, rhs_start, 0)

    load_links.wait()
    load_owner.wait()
    build_operator(links, weights)

    def rhs_wait(i, carry):
        at = i // n_group
        source = lax.rem(g + i, n_group)
        pltpu.make_async_remote_copy(
            src_ref=rhs_out,
            dst_ref=rhs_in.at[at, source],
            send_sem=rhs_send.at[i],
            recv_sem=rhs_recv.at[at, source],
            device_id=device(0, 1),
            device_id_type=MESH,
        ).wait_recv()
        return carry

    lax.fori_loop(1, n_far + 1, rhs_wait, 0)

    def chosen(at, x):
        picked = jnp.zeros((8, 128), F32)
        for k in range(n_group):
            picked = picked + jnp.where(owner[k] == x, rhs_in[at, k].astype(F32), 0.0)
        return picked

    ahead_x = lax.rem(g + 1, n_group)
    behind_x = lax.rem(g + n_group - 1, n_group)
    rhs = chosen(0, g)
    others = [chosen(0, ahead_x), chosen(0, behind_x), chosen(1, g), chosen(2, g)]
    iterate = rhs - hop(weights, rhs, others, row)

    steps = [(n_group - 1, 0), (1, 0), (0, n_sub - 1), (0, 1)]
    pending = []
    for step in range(COARSE_STEPS - 1):
        iter_out[step] = iterate
        copies = [
            pltpu.make_async_remote_copy(
                src_ref=iter_out.at[step],
                dst_ref=iter_in.at[step, way],
                send_sem=iter_send.at[step, way],
                recv_sem=iter_recv.at[step, way],
                device_id=device(*steps[way]),
                device_id_type=MESH,
            )
            for way in range(4)
        ]
        for copy in copies:
            copy.start()
        for copy in copies:
            copy.wait_recv()
        pending += copies
        iterate = rhs - hop(weights, iterate, [iter_in[step, way] for way in range(4)], row)

    rounded = iterate.astype(BF16)
    last_out[...] = rounded
    last_in[g] = rounded

    def last_copy(i, at):
        return pltpu.make_async_remote_copy(
            src_ref=last_out,
            dst_ref=last_in.at[at],
            send_sem=last_send.at[i],
            recv_sem=last_recv.at[at],
            device_id=device(i, 0),
            device_id_type=MESH,
        )

    def last_start(i, carry):
        last_copy(i, g).start()
        return carry

    lax.fori_loop(1, n_group, last_start, 0)
    sol_ref[...] = iterate

    def last_wait(i, carry):
        last_copy(i, lax.rem(g + i, n_group)).wait_recv()
        return carry

    lax.fori_loop(1, n_group, last_wait, 0)

    block_here = jnp.int32(0)
    for k in range(n_group):
        block_here = block_here + jnp.where(g == k, owner[k], 0)
    own = jnp.zeros((8, 128), F32)
    for k in range(n_group):
        own = own + jnp.where(block_here == k, last_in[k].astype(F32), 0.0)

    own_ref[...] = own

    def rhs_done(i, carry):
        rhs_copy(i).wait_send()
        return carry

    lax.fori_loop(1, n_far + 1, rhs_done, 0)
    for copy in pending:
        copy.wait_send()

    def last_done(i, carry):
        last_copy(i, g).wait_send()
        return carry

    lax.fori_loop(1, n_group, last_done, 0)


def on_device(n_group, n_sub, fine_residual, null_vectors, agg_map, block_owner, coarse_links):
    hbm = pl.BlockSpec(memory_space=pltpu.HBM)
    vmem = pl.BlockSpec(memory_space=pltpu.VMEM)
    dma = pltpu.SemaphoreType.DMA
    exchanges = COARSE_STEPS - 1
    in_hbm = functools.partial(pltpu.with_memory_space_constraint, memory_space=pltpu.HBM)
    solved = pl.pallas_call(
        functools.partial(kernel, n_group, n_sub),
        out_shape=(
            jax.ShapeDtypeStruct((8, 128), F32),
            jax.ShapeDtypeStruct((8, 128), F32),
            jax.ShapeDtypeStruct((NAGG, FS), F32),
            jax.ShapeDtypeStruct((2, SPIN_COLOR, NULLV, FS), BF16),
        ),
        in_specs=[hbm] * 5,
        out_specs=(vmem,) * 4,
        scratch_shapes=[
            pltpu.VMEM((2, SPIN_COLOR, RHS, FS), BF16),
            pltpu.VMEM((1, FS), jnp.int32),
            pltpu.VMEM((36, CDOF, CDOF), BF16),
            pltpu.SMEM((n_group,), jnp.int32),
            pltpu.VMEM((6 * 128, 256), BF16),
            pltpu.VMEM((8, 128), BF16),
            pltpu.VMEM((3, n_group, 8, 128), BF16),
            pltpu.VMEM((exchanges, 8, 128), F32),
            pltpu.VMEM((exchanges, 4, 8, 128), F32),
            pltpu.VMEM((8, 128), BF16),
            pltpu.VMEM((n_group, 8, 128), BF16),
            dma((4 + NBLOCK,)),
            dma((3 * n_group,)),
            dma((3, n_group)),
            dma((exchanges, 4)),
            dma((exchanges, 4)),
            dma((n_group,)),
            dma((n_group,)),
        ],
        compiler_params=pltpu.CompilerParams(
            collective_id=0, has_side_effects=True, vmem_limit_bytes=24 * 1024 * 1024
        ),
        name="coarse",
    )(
        in_hbm(block_owner),
        in_hbm(fine_residual),
        in_hbm(null_vectors),
        in_hbm(agg_map),
        in_hbm(coarse_links.reshape(36, CDOF, CDOF)),
    )
    solution_here, correction = pl.pallas_call(
        prolong_kernel,
        out_shape=(
            jax.ShapeDtypeStruct((2, 2, RHS, CDOF), F32),
            jax.ShapeDtypeStruct((2, SPIN_COLOR, RHS, FS), BF16),
        ),
        in_specs=[vmem] * 4,
        out_specs=(hbm, hbm),
        scratch_shapes=[
            pltpu.VMEM((2, 2, RHS, CDOF), F32),
            pltpu.VMEM((2, SPIN_COLOR, RHS, FS), BF16),
            dma((1 + NBLOCK,)),
        ],
        compiler_params=pltpu.CompilerParams(vmem_limit_bytes=24 * 1024 * 1024),
        name="prolong",
    )(*solved)
    return solution_here.reshape(1, 1, 2, 2, RHS, CDOF), correction


def solution(mesh):
    in_specs = (
        P(None, None, None, ("group", "sub")),
        P(None, None, None, ("group", "sub")),
        P(("group", "sub"), None),
        P(),
        P(None, "group", "sub", None, None, None, None),
    )
    out_specs = (P("group", "sub", None, None, None, None), P(None, None, None, ("group", "sub")))
    return jax.shard_map(
        functools.partial(on_device, mesh.shape["group"], mesh.shape["sub"]),
        mesh=mesh,
        in_specs=in_specs,
        out_specs=out_specs,
        check_vma=False,
    )
```

```python
import functools

import jax
import jax.numpy as jnp
from jax import lax
from jax.experimental import pallas as pl
from jax.experimental.pallas import tpu as pltpu
from jax.sharding import PartitionSpec as P

SPIN_COLOR = 12
NULLV = 32
AGG = 256
COARSE_STEPS = 4
RHS = 4
CDOF = 64
NAGG = 4
FS = NAGG * AGG
FBLOCK = 4
NBLOCK = SPIN_COLOR // FBLOCK
MESH = pl.DeviceIdType.MESH
F32 = jnp.float32
BF16 = jnp.bfloat16


def site_masks(agg_row):
    high = agg_row // 128
    low = agg_row % 128
    lanes = lax.broadcasted_iota(jnp.int32, (128, FS), 0)
    low_hot = jnp.where(lanes == low, 1.0, 0.0).astype(BF16)
    row = lax.broadcasted_iota(jnp.int32, (32, FS), 0)
    place = lax.broadcasted_iota(jnp.int32, (32, FS), 1)
    high_hot = jnp.where((row % 8 == high) & (row // 8 == place // AGG), 1.0, 0.0).astype(BF16)
    grid = lax.dot_general(
        high_hot, low_hot, (((1,), (1,)), ((), ())), preferred_element_type=F32
    )
    return [
        jnp.concatenate([grid[a * 8 + h : a * 8 + h + 1] for h in range(8)], axis=1)
        for a in range(NAGG)
    ]


def fold_lanes(tile):
    tile = tile + pltpu.roll(tile, 64, 1)
    return tile + pltpu.roll(tile, 32, 1)


def restricted_piece(total, row, lane):
    per_agg = []
    for a in range(NAGG):
        parts = []
        for ri in range(2):
            kept = jnp.zeros((8, 128), F32)
            for f in range(FBLOCK):
                at = (f * NAGG + a) * 8
                tile = total[at : at + 8, ri * 128 : (ri + 1) * 128]
                kept = kept + jnp.where(lane // NULLV == f, tile, 0.0)
            parts.append(fold_lanes(kept))
        by_re, by_im = parts
        real = by_re + pltpu.roll(by_im, 4, 0)
        imag = pltpu.roll(by_re, 4, 0) - by_im
        per_agg.append(jnp.where((lane // NULLV) % 2 == 0, real, imag))
    upper = jnp.where(lane < CDOF, per_agg[0], per_agg[1])
    lower = jnp.where(lane < CDOF, per_agg[2], per_agg[3])
    return jnp.where(row < 4, upper, pltpu.roll(lower, 4, 0))


def restrict(fine, null, masks, row, lane, loads=()):
    total = jnp.zeros((128, 256), F32)
    for b in range(NBLOCK):
        spread = []
        for f in range(b * FBLOCK, (b + 1) * FBLOCK):
            psi = jnp.concatenate([fine[0, f].astype(F32), fine[1, f].astype(F32)], axis=0)
            spread += [psi * masks[a] for a in range(NAGG)]
        spread = jnp.concatenate(spread, axis=0).astype(BF16)
        for load in loads[b : b + 1]:
            load.wait()
        part = null[:, b * FBLOCK : (b + 1) * FBLOCK].reshape(2 * FBLOCK * NULLV, FS)
        total = total + lax.dot_general(
            spread, part, (((1,), (1,)), ((), ())), preferred_element_type=F32
        )
    return restricted_piece(total, row, lane)


def prolongation_rows(piece, row, lane):
    block = lane // NULLV
    swapped = pltpu.roll(piece, 4, 0)
    doubled = (jnp.where(row < 4, piece, swapped), jnp.where(row < 4, swapped, piece))
    rows = []
    for y in range(2):
        for z in range(2):
            re, im = (
                fold_lanes(jnp.where(block == 2 * z + part, doubled[y], 0.0)) for part in range(2)
            )
            for left, right in ((re, -im), (im, re)):
                for pair in range(2):
                    same = block == 2 * pair + row // RHS
                    rows.append(
                        jnp.concatenate(
                            [jnp.where(same, left, 0.0), jnp.where(same, right, 0.0)], axis=1
                        )
                    )
    return jnp.concatenate(rows, axis=0).astype(BF16)


def prolong_kernel(sol_ref, own_ref, masks_ref, null, sol_out, corr_out, sol, corr, sem):
    row = lax.broadcasted_iota(jnp.int32, (8, 128), 0)
    lane = lax.broadcasted_iota(jnp.int32, (8, 128), 1)
    for y in range(2):
        for z in range(2):
            sol[y, z] = sol_ref[y * RHS : (y + 1) * RHS, z * CDOF : (z + 1) * CDOF]
    stores = [pltpu.make_async_copy(sol, sol_out, sem.at[NBLOCK])]
    stores[0].start()
    left = prolongation_rows(own_ref[...], row, lane)
    for b in range(NBLOCK):
        at_f = pl.ds(b * FBLOCK, FBLOCK)
        part = null[:, b * FBLOCK : (b + 1) * FBLOCK].reshape(2 * FBLOCK * NULLV, FS)
        wide = jnp.dot(left, part, preferred_element_type=F32)
        here = wide[:32] * masks_ref[0:1]
        for a in range(1, NAGG):
            here = here + wide[a * 32 : (a + 1) * 32] * masks_ref[a : a + 1]
        for ri in range(2):
            for f in range(FBLOCK):
                at = (ri * FBLOCK + f) * RHS
                corr[ri, b * FBLOCK + f] = here[at : at + RHS].astype(BF16)
        stores.append(
            pltpu.make_async_copy(corr.at[:, at_f], corr_out.at[:, at_f], sem.at[b])
        )
        stores[-1].start()
    for store in stores:
        store.wait()


def build_operator(links, weights):
    zero = jnp.zeros((CDOF, CDOF), BF16)

    def sited(block, z):
        return jnp.concatenate([block, zero] if z == 0 else [zero, block], axis=1)

    for y in range(2):
        for z in range(2):
            n = 2 * y + z
            here = links[0 * 4 + n]
            across = links[(7 + z) * 4 + n]
            columns = [
                jnp.concatenate([here, across] if z == 0 else [across, here], axis=1),
                sited(links[(5 + y) * 4 + n], z),
            ] + [sited(links[k * 4 + n], z) for k in (1, 2, 3, 4)]
            for source, column in enumerate(columns):
                weights[source * 128 : (source + 1) * 128, n * CDOF : (n + 1) * CDOF] = column.T


def hop(weights, here, others, row):
    low = [here, pltpu.roll(here, 4, 0)] + list(others)
    low = jnp.concatenate(low, axis=1).astype(BF16)
    out = jnp.dot(low, weights[: len(others) * 128 + 256], preferred_element_type=F32)
    return jnp.where(row < 4, out[:, :128], out[:, 128:])


def pushes(toward, here, row, lane):
    low = jnp.concatenate([jnp.where(lane < CDOF, here, 0.0), jnp.where(lane < CDOF, 0.0, here)], axis=0)
    out = jnp.dot(low.astype(BF16), toward[...], preferred_element_type=F32)
    parts = []
    for k in range(4):
        low_z, high_z = out[:8, k * 128 : (k + 1) * 128], out[8:, k * 128 : (k + 1) * 128]
        low_z = jnp.where(row < 4, low_z, pltpu.roll(low_z, CDOF, 1))
        high_z = jnp.where(row < 4, pltpu.roll(high_z, CDOF, 1), high_z)
        parts.append(jnp.where(lane < CDOF, low_z, high_z))
    return parts


def kernel(
    n_group,
    n_sub,
    owner_ref,
    fine_ref,
    null_ref,
    agg_ref,
    links_ref,
    sol_ref,
    own_ref,
    masks_ref,
    null,
    fine,
    agg,
    links,
    owner,
    weights,
    toward,
    link_out,
    link_in,
    rhs_out,
    rhs_in,
    near_out,
    near_in,
    far_out,
    far_in,
    skew_out,
    skew_in,
    last_out,
    last_in,
    turn_out,
    turn_in,
    local_sem,
    link_send,
    link_recv,
    rhs_send,
    rhs_recv,
    mid_send,
    mid_recv,
    last_send,
    last_recv,
):
    g = lax.axis_index("group")
    s = lax.axis_index("sub")
    half = n_group // 2
    chips = n_group // 4
    at_x, at_y, at_core = g // 4, (g // 2) % 2, g % 2

    def device(dg, ds):
        return lax.rem(g + (dg + n_group), n_group), lax.rem(s + (ds + n_sub), n_sub)

    def member(flip, i):
        x = lax.rem(at_x + (chips - 1 - i // 2), chips)
        return x * 4 + lax.rem(at_y + flip, 2) * 2 + lax.rem(at_core + 1 - i % 2, 2)

    def remote(src, dst, send, recv, to):
        return pltpu.make_async_remote_copy(
            src_ref=src, dst_ref=dst, send_sem=send, recv_sem=recv, device_id=to, device_id_type=MESH
        )

    def each(count, body):
        def run(i, carry):
            body(i)
            return carry

        lax.fori_loop(0, count, run, 0)

    load_agg = pltpu.make_async_copy(agg_ref, agg, local_sem.at[0])
    load_fine = pltpu.make_async_copy(fine_ref, fine, local_sem.at[1])
    load_links = pltpu.make_async_copy(links_ref, links, local_sem.at[2])
    load_null = [
        pltpu.make_async_copy(
            null_ref.at[:, pl.ds(b * FBLOCK, FBLOCK)],
            null.at[:, pl.ds(b * FBLOCK, FBLOCK)],
            local_sem.at[3 + b],
        )
        for b in range(NBLOCK)
    ]
    load_owner = pltpu.make_async_copy(owner_ref, owner, local_sem.at[3 + NBLOCK])
    load_agg.start()
    load_fine.start()
    for load in load_null:
        load.start()
    load_links.start()
    load_owner.start()

    to_t = (0, -1, 1)
    barrier = pltpu.get_barrier_semaphore()

    def greet(to):
        pl.semaphore_signal(barrier, inc=1, device_id=to, device_id_type=MESH)

    for at in (2, 1, 0):
        for flip in (1, 0):
            count = half - 1 if at == 0 and flip == 0 else half
            each(count, lambda i: greet((member(flip, i), device(0, to_t[at])[1])))
    greet(device(0, 2))
    greet(device(0, -2))

    row = lax.broadcasted_iota(jnp.int32, (8, 128), 0)
    lane = lax.broadcasted_iota(jnp.int32, (8, 128), 1)

    load_agg.wait()
    masks = site_masks(agg[...])
    for a in range(NAGG):
        masks_ref[a : a + 1] = masks[a]
    load_fine.wait()
    mine = restrict(fine, null, masks, row, lane, load_null).astype(BF16)
    rhs_out[...] = mine
    rhs_in[0, g] = mine

    pl.semaphore_wait(barrier, 3 * n_group - 1 + 2)

    def rhs_copy(at, flip, i):
        return remote(
            rhs_out,
            rhs_in.at[at, g],
            rhs_send.at[at, flip * half + i],
            rhs_recv.at[at, g],
            (member(flip, i), device(0, to_t[at])[1]),
        )

    broadcast = [
        (at, flip, half - 1 if at == 0 and flip == 0 else half) for flip in (1, 0) for at in (2, 1, 0)
    ]
    for at, flip, count in broadcast:
        each(count, lambda i: rhs_copy(at, flip, i).start())

    ahead = ((1, 0), (-1, 0), (0, 1), (0, -1))
    load_links.wait()
    link_copies = []
    for k in range(4):
        for y in range(2):
            at = (k + 1) * 4 + 2 * y
            link_out[k, y * CDOF : (y + 1) * CDOF] = jnp.concatenate(
                [links[at], links[at + 1]], axis=1
            )
        copy = remote(
            link_out.at[k], link_in.at[k], link_send.at[k], link_recv.at[k], device(*ahead[k])
        )
        copy.start()
        link_copies.append(copy)
    build_operator(links, weights)
    load_owner.wait()
    for k, copy in enumerate(link_copies):
        copy.wait_recv()
        toward[:, k * 128 : (k + 1) * 128] = link_in[k].T

    def rhs_wait(at, flip, i):
        source = member(flip, i)
        remote(
            rhs_out, rhs_in.at[at, source], rhs_send.at[at, 0], rhs_recv.at[at, source], device(0, 1)
        ).wait_recv()

    for at, flip, count in broadcast:
        each(count, lambda i: rhs_wait(at, flip, i))

    def chosen(at, x):
        picked = jnp.zeros((8, 128), F32)
        for k in range(n_group):
            picked = picked + jnp.where(owner[k] == x, rhs_in[at, k].astype(F32), 0.0)
        return picked

    ahead_x, behind_x = device(1, 0)[0], device(-1, 0)[0]
    rhs = chosen(0, g)
    others = [chosen(0, ahead_x), chosen(0, behind_x), chosen(1, g), chosen(2, g)]
    first = rhs - hop(weights, rhs, others, row)

    near_out[0] = first.astype(BF16)
    near_out[1] = (rhs - hop(weights, first, [], row)).astype(BF16)
    pushed = pushes(toward, first, row, lane)
    pairs = [(kx, kt) for kx in (0, 1) for kt in (2, 3)]
    for at, pair in enumerate(pairs):
        for side in range(2):
            skew_out[at, side] = pushed[pair[side]].astype(BF16)
    for k in range(4):
        far_out[k] = pushed[k].astype(BF16)

    def back(*ks):
        return device(-sum(ahead[k][0] for k in ks), -sum(ahead[k][1] for k in ks))

    mid_copies = (
        [
            remote(skew_out.at[at], skew_in.at[at], mid_send.at[8 + at], mid_recv.at[8 + at], back(*pair))
            for at, pair in enumerate(pairs)
        ]
        + [
            remote(near_out, near_in.at[k], mid_send.at[k], mid_recv.at[k], back(k))
            for k in range(4)
        ]
        + [
            remote(far_out.at[k], far_in.at[k], mid_send.at[4 + k], mid_recv.at[4 + k], back(k, k))
            for k in range(4)
        ]
    )
    for copy in mid_copies:
        copy.start()
    for copy in mid_copies:
        copy.wait_recv()
    second = rhs - hop(weights, first, [near_in[k, 0].astype(F32) for k in range(4)], row)
    around = []
    for k in range(4):
        value = near_in[k, 1].astype(F32) - far_in[k].astype(F32) - pushed[k ^ 1]
        for at, pair in enumerate(pairs):
            if k in pair:
                value = value - skew_in[at, 1 - pair.index(k)].astype(F32)
        around.append(value)
    third = rhs - hop(weights, second, around, row)

    part = rhs - hop(weights, third, [], row)
    pushed = pushes(toward, third, row, lane)
    for at, piece in enumerate((part, pushed[0], pushed[1])):
        last_out[at] = piece.astype(BF16)
        last_in[g, at] = piece.astype(BF16)
    turn_out[0] = pushed[2].astype(BF16)
    turn_out[1] = pushed[3].astype(BF16)

    def last_copy(at, flip, i, source):
        src = last_out if at == 0 else turn_out.at[at - 1]
        dst = last_in.at[source] if at == 0 else turn_in.at[at - 1, source]
        return remote(
            src,
            dst,
            last_send.at[at, flip * half + i],
            last_recv.at[at, source],
            (member(flip, i), device(0, to_t[at])[1]),
        )

    for at, flip, count in broadcast:
        each(count, lambda i: last_copy(at, flip, i, g).start())
    block_here = jnp.int32(0)
    for k in range(n_group):
        block_here = block_here + jnp.where(g == k, owner[k], 0)
    for at, flip, count in broadcast:
        each(count, lambda i: last_copy(at, flip, i, member(flip, i)).wait_recv())

    def gathered(start, x):
        after, before = lax.rem(x + 1, n_group), lax.rem(x + n_group - 1, n_group)
        value = start
        for k in range(n_group):
            if start is None:
                mine = last_in[k, 0].astype(F32)
                mine = mine - turn_in[0, k].astype(F32) - turn_in[1, k].astype(F32)
                value = jnp.where(x == k, mine, 0.0) + (0.0 if value is None else value)
            else:
                mine = turn_in[0, k].astype(F32) + turn_in[1, k].astype(F32)
                value = value - jnp.where(x == k, mine, 0.0)
            value = value - jnp.where(after == k, last_in[k, 1].astype(F32), 0.0)
            value = value - jnp.where(before == k, last_in[k, 2].astype(F32), 0.0)
        return value

    sol_ref[...] = gathered(part, g)
    own_ref[...] = gathered(None, block_here).astype(BF16).astype(F32)

    for copy in link_copies + mid_copies:
        copy.wait_send()
    for at, flip, count in broadcast:
        each(count, lambda i: rhs_copy(at, flip, i).wait_send())
        each(count, lambda i: last_copy(at, flip, i, g).wait_send())


def on_device(n_group, n_sub, fine_residual, null_vectors, agg_map, block_owner, coarse_links):
    hbm = pl.BlockSpec(memory_space=pltpu.HBM)
    vmem = pl.BlockSpec(memory_space=pltpu.VMEM)
    dma = pltpu.SemaphoreType.DMA

    def piece(*lead):
        return pltpu.VMEM((*lead, 8, 128), BF16)

    in_hbm = functools.partial(pltpu.with_memory_space_constraint, memory_space=pltpu.HBM)
    solved = pl.pallas_call(
        functools.partial(kernel, n_group, n_sub),
        out_shape=(
            jax.ShapeDtypeStruct((8, 128), F32),
            jax.ShapeDtypeStruct((8, 128), F32),
            jax.ShapeDtypeStruct((NAGG, FS), F32),
            jax.ShapeDtypeStruct((2, SPIN_COLOR, NULLV, FS), BF16),
        ),
        in_specs=[hbm] * 5,
        out_specs=(vmem,) * 4,
        scratch_shapes=[
            pltpu.VMEM((2, SPIN_COLOR, RHS, FS), BF16),
            pltpu.VMEM((1, FS), jnp.int32),
            pltpu.VMEM((36, CDOF, CDOF), BF16),
            pltpu.SMEM((n_group,), jnp.int32),
            pltpu.VMEM((6 * 128, 256), BF16),
            pltpu.VMEM((128, 4 * 128), BF16),
            pltpu.VMEM((4, 128, 128), BF16),
            pltpu.VMEM((4, 128, 128), BF16),
            piece(),
            piece(3, n_group),
            piece(2),
            piece(4, 2),
            piece(4),
            piece(4),
            piece(4, 2),
            piece(4, 2),
            piece(3),
            piece(n_group, 3),
            piece(2),
            piece(2, n_group),
            dma((4 + NBLOCK,)),
            dma((4,)),
            dma((4,)),
            dma((3, n_group)),
            dma((3, n_group)),
            dma((12,)),
            dma((12,)),
            dma((3, n_group)),
            dma((3, n_group)),
        ],
        compiler_params=pltpu.CompilerParams(
            collective_id=0, has_side_effects=True, vmem_limit_bytes=24 * 1024 * 1024
        ),
        name="coarse",
    )(
        in_hbm(block_owner),
        in_hbm(fine_residual),
        in_hbm(null_vectors),
        in_hbm(agg_map),
        in_hbm(coarse_links.reshape(36, CDOF, CDOF)),
    )
    solution_here, correction = pl.pallas_call(
        prolong_kernel,
        out_shape=(
            jax.ShapeDtypeStruct((2, 2, RHS, CDOF), F32),
            jax.ShapeDtypeStruct((2, SPIN_COLOR, RHS, FS), BF16),
        ),
        in_specs=[vmem] * 4,
        out_specs=(hbm, hbm),
        scratch_shapes=[
            pltpu.VMEM((2, 2, RHS, CDOF), F32),
            pltpu.VMEM((2, SPIN_COLOR, RHS, FS), BF16),
            dma((1 + NBLOCK,)),
        ],
        compiler_params=pltpu.CompilerParams(vmem_limit_bytes=24 * 1024 * 1024),
        name="prolong",
    )(*solved)
    return solution_here.reshape(1, 1, 2, 2, RHS, CDOF), correction


def solution(mesh):
    in_specs = (
        P(None, None, None, ("group", "sub")),
        P(None, None, None, ("group", "sub")),
        P(("group", "sub"), None),
        P(),
        P(None, "group", "sub", None, None, None, None),
    )
    out_specs = (P("group", "sub", None, None, None, None), P(None, None, None, ("group", "sub")))
    return jax.shard_map(
        functools.partial(on_device, mesh.shape["group"], mesh.shape["sub"]),
        mesh=mesh,
        in_specs=in_specs,
        out_specs=out_specs,
        check_vma=False,
    )
```

```python
import functools

import jax
import jax.numpy as jnp
from jax import lax
from jax.experimental import pallas as pl
from jax.experimental.pallas import tpu as pltpu
from jax.sharding import PartitionSpec as P

SPIN_COLOR = 12
NULLV = 32
AGG = 256
COARSE_STEPS = 4
RHS = 4
CDOF = 64
NAGG = 4
FS = NAGG * AGG
FBLOCK = 4
NBLOCK = SPIN_COLOR // FBLOCK
MESH = pl.DeviceIdType.MESH
F32 = jnp.float32
BF16 = jnp.bfloat16


def site_masks(agg_row):
    high = agg_row // 128
    low = agg_row % 128
    lanes = lax.broadcasted_iota(jnp.int32, (128, FS), 0)
    low_hot = jnp.where(lanes == low, 1.0, 0.0).astype(BF16)
    row = lax.broadcasted_iota(jnp.int32, (32, FS), 0)
    place = lax.broadcasted_iota(jnp.int32, (32, FS), 1)
    high_hot = jnp.where((row % 8 == high) & (row // 8 == place // AGG), 1.0, 0.0).astype(BF16)
    grid = lax.dot_general(
        high_hot, low_hot, (((1,), (1,)), ((), ())), preferred_element_type=F32
    )
    return [
        jnp.concatenate([grid[a * 8 + h : a * 8 + h + 1] for h in range(8)], axis=1)
        for a in range(NAGG)
    ]


def fold_lanes(tile):
    tile = tile + pltpu.roll(tile, 64, 1)
    return tile + pltpu.roll(tile, 32, 1)


def restricted_piece(total, row, lane):
    per_agg = []
    for a in range(NAGG):
        parts = []
        for ri in range(2):
            kept = jnp.zeros((8, 128), F32)
            for f in range(FBLOCK):
                at = (f * NAGG + a) * 8
                tile = total[at : at + 8, ri * 128 : (ri + 1) * 128]
                kept = kept + jnp.where(lane // NULLV == f, tile, 0.0)
            parts.append(fold_lanes(kept))
        by_re, by_im = parts
        real = by_re + pltpu.roll(by_im, 4, 0)
        imag = pltpu.roll(by_re, 4, 0) - by_im
        per_agg.append(jnp.where((lane // NULLV) % 2 == 0, real, imag))
    upper = jnp.where(lane < CDOF, per_agg[0], per_agg[1])
    lower = jnp.where(lane < CDOF, per_agg[2], per_agg[3])
    return jnp.where(row < 4, upper, pltpu.roll(lower, 4, 0))


def restrict(fine, null, masks, row, lane, loads=()):
    total = jnp.zeros((128, 256), F32)
    for b in range(NBLOCK):
        spread = []
        for f in range(b * FBLOCK, (b + 1) * FBLOCK):
            psi = jnp.concatenate([fine[0, f].astype(F32), fine[1, f].astype(F32)], axis=0)
            spread += [psi * masks[a] for a in range(NAGG)]
        spread = jnp.concatenate(spread, axis=0).astype(BF16)
        for load in loads[b : b + 1]:
            load.wait()
        part = null[:, b * FBLOCK : (b + 1) * FBLOCK].reshape(2 * FBLOCK * NULLV, FS)
        total = total + lax.dot_general(
            spread, part, (((1,), (1,)), ((), ())), preferred_element_type=F32
        )
    return restricted_piece(total, row, lane)


def prolongation_rows(piece, row, lane):
    block = lane // NULLV
    swapped = pltpu.roll(piece, 4, 0)
    doubled = (jnp.where(row < 4, piece, swapped), jnp.where(row < 4, swapped, piece))
    rows = []
    for y in range(2):
        for z in range(2):
            re, im = (
                fold_lanes(jnp.where(block == 2 * z + part, doubled[y], 0.0)) for part in range(2)
            )
            for left, right in ((re, -im), (im, re)):
                for pair in range(2):
                    same = block == 2 * pair + row // RHS
                    rows.append(
                        jnp.concatenate(
                            [jnp.where(same, left, 0.0), jnp.where(same, right, 0.0)], axis=1
                        )
                    )
    return jnp.concatenate(rows, axis=0).astype(BF16)


def prolong_kernel(sol_ref, own_ref, masks_ref, null, sol_out, corr_out, sol, corr, sem):
    row = lax.broadcasted_iota(jnp.int32, (8, 128), 0)
    lane = lax.broadcasted_iota(jnp.int32, (8, 128), 1)
    for y in range(2):
        for z in range(2):
            sol[y, z] = sol_ref[y * RHS : (y + 1) * RHS, z * CDOF : (z + 1) * CDOF]
    stores = [pltpu.make_async_copy(sol, sol_out, sem.at[NBLOCK])]
    stores[0].start()
    left = prolongation_rows(own_ref[...], row, lane)
    for b in range(NBLOCK):
        at_f = pl.ds(b * FBLOCK, FBLOCK)
        part = null[:, b * FBLOCK : (b + 1) * FBLOCK].reshape(2 * FBLOCK * NULLV, FS)
        wide = jnp.dot(left, part, preferred_element_type=F32)
        here = wide[:32] * masks_ref[0:1]
        for a in range(1, NAGG):
            here = here + wide[a * 32 : (a + 1) * 32] * masks_ref[a : a + 1]
        for ri in range(2):
            for f in range(FBLOCK):
                at = (ri * FBLOCK + f) * RHS
                corr[ri, b * FBLOCK + f] = here[at : at + RHS].astype(BF16)
        stores.append(
            pltpu.make_async_copy(corr.at[:, at_f], corr_out.at[:, at_f], sem.at[b])
        )
        stores[-1].start()
    for store in stores:
        store.wait()


def build_operator(links, weights):
    zero = jnp.zeros((CDOF, CDOF), BF16)

    def sited(block, z):
        return jnp.concatenate([block, zero] if z == 0 else [zero, block], axis=1)

    for y in range(2):
        for z in range(2):
            n = 2 * y + z
            here = links[0 * 4 + n]
            across = links[(7 + z) * 4 + n]
            columns = [
                jnp.concatenate([here, across] if z == 0 else [across, here], axis=1),
                sited(links[(5 + y) * 4 + n], z),
            ] + [sited(links[k * 4 + n], z) for k in (1, 2, 3, 4)]
            for source, column in enumerate(columns):
                weights[source * 128 : (source + 1) * 128, n * CDOF : (n + 1) * CDOF] = column.T


def hop(weights, here, others, row):
    low = [here, pltpu.roll(here, 4, 0)] + list(others)
    low = jnp.concatenate(low, axis=1).astype(BF16)
    out = jnp.dot(low, weights[: len(others) * 128 + 256], preferred_element_type=F32)
    return jnp.where(row < 4, out[:, :128], out[:, 128:])


def pushes(toward, here, row, lane):
    low = jnp.concatenate([jnp.where(lane < CDOF, here, 0.0), jnp.where(lane < CDOF, 0.0, here)], axis=0)
    out = jnp.dot(low.astype(BF16), toward[...], preferred_element_type=F32)
    parts = []
    for k in range(4):
        low_z, high_z = out[:8, k * 128 : (k + 1) * 128], out[8:, k * 128 : (k + 1) * 128]
        low_z = jnp.where(row < 4, low_z, pltpu.roll(low_z, CDOF, 1))
        high_z = jnp.where(row < 4, pltpu.roll(high_z, CDOF, 1), high_z)
        parts.append(jnp.where(lane < CDOF, low_z, high_z))
    return parts


def kernel(
    n_group,
    n_sub,
    owner_ref,
    fine_ref,
    null_ref,
    agg_ref,
    links_ref,
    sol_ref,
    own_ref,
    masks_ref,
    null,
    fine,
    agg,
    links,
    owner,
    weights,
    toward,
    link_out,
    link_in,
    rhs_out,
    rhs_in,
    near_out,
    far_out,
    skew_out,
    mid_in,
    last_out,
    last_in,
    turn_out,
    turn_in,
    local_sem,
    link_send,
    link_recv,
    rhs_send,
    rhs_recv,
    mid_send,
    mid_recv,
    last_send,
    last_recv,
    turn_send,
    turn_recv,
):
    g = lax.axis_index("group")
    s = lax.axis_index("sub")
    half = n_group // 2
    chips = n_group // 4
    at_x, at_y, at_core = g // 4, (g // 2) % 2, g % 2

    def device(dg, ds):
        return lax.rem(g + (dg + n_group), n_group), lax.rem(s + (ds + n_sub), n_sub)

    def member(flip, i):
        x = lax.rem(at_x + (chips - 1 - i // 2), chips)
        return x * 4 + lax.rem(at_y + flip, 2) * 2 + lax.rem(at_core + 1 - i % 2, 2)

    def remote(src, dst, send, recv, to):
        return pltpu.make_async_remote_copy(
            src_ref=src, dst_ref=dst, send_sem=send, recv_sem=recv, device_id=to, device_id_type=MESH
        )

    def each(count, body):
        for i in range(count):
            body(i)

    def arrived(buffer, sem):
        pltpu.make_async_copy(buffer, buffer, sem).wait()

    load_agg = pltpu.make_async_copy(agg_ref, agg, local_sem.at[0])
    load_fine = pltpu.make_async_copy(fine_ref, fine, local_sem.at[1])
    load_links = pltpu.make_async_copy(links_ref, links, local_sem.at[2])
    load_null = [
        pltpu.make_async_copy(
            null_ref.at[:, pl.ds(b * FBLOCK, FBLOCK)],
            null.at[:, pl.ds(b * FBLOCK, FBLOCK)],
            local_sem.at[3 + b],
        )
        for b in range(NBLOCK)
    ]
    load_owner = pltpu.make_async_copy(owner_ref, owner, local_sem.at[3 + NBLOCK])
    to_t = (0, -1, 1)
    barrier = pltpu.get_barrier_semaphore()

    def greet(to):
        pl.semaphore_signal(barrier, inc=1, device_id=to, device_id_type=MESH)

    for flip in (1, 0):
        for at in (2, 1, 0):
            count = half - 1 if at == 0 and flip == 0 else half
            each(count, lambda i: greet((member(flip, i), device(0, to_t[at])[1])))
    greet(device(0, 2))
    greet(device(0, -2))

    load_agg.start()
    load_fine.start()
    for load in load_null:
        load.start()
    load_links.start()
    load_owner.start()

    row = lax.broadcasted_iota(jnp.int32, (8, 128), 0)
    lane = lax.broadcasted_iota(jnp.int32, (8, 128), 1)

    load_agg.wait()
    masks = site_masks(agg[...])
    for a in range(NAGG):
        masks_ref[a : a + 1] = masks[a]
    load_fine.wait()
    mine = restrict(fine, null, masks, row, lane, load_null).astype(BF16)
    rhs_out[...] = mine
    keep_rhs = pltpu.make_async_copy(rhs_out, rhs_in.at[0, g], rhs_recv)
    keep_rhs.start()

    pl.semaphore_wait(barrier, 3 * n_group - 1 + 2)

    def rhs_copy(at, flip, i):
        return remote(
            rhs_out,
            rhs_in.at[at, g],
            rhs_send,
            rhs_recv,
            (member(flip, i), device(0, to_t[at])[1]),
        )

    broadcast = [
        (at, flip, half - 1 if at == 0 and flip == 0 else half) for flip in (1, 0) for at in (2, 1, 0)
    ]
    for at, flip, count in broadcast:
        each(count, lambda i: rhs_copy(at, flip, i).start())

    ahead = ((1, 0), (-1, 0), (0, 1), (0, -1))
    load_links.wait()
    for k in range(4):
        for y in range(2):
            at = (k + 1) * 4 + 2 * y
            link_out[k, y * CDOF : (y + 1) * CDOF] = jnp.concatenate(
                [links[at], links[at + 1]], axis=1
            )
        copy = remote(
            link_out.at[k], link_in.at[k], link_send, link_recv, device(*ahead[k])
        )
        copy.start()
    build_operator(links, weights)
    load_owner.wait()
    arrived(link_in, link_recv)
    for k in range(4):
        toward[:, k * 128 : (k + 1) * 128] = link_in[k].T

    arrived(rhs_in, rhs_recv)

    def chosen(at, x):
        picked = jnp.zeros((8, 128), F32)
        for k in range(n_group):
            picked = picked + jnp.where(owner[k] == x, rhs_in[at, k].astype(F32), 0.0)
        return picked

    ahead_x, behind_x = device(1, 0)[0], device(-1, 0)[0]
    rhs = chosen(0, g)
    others = [chosen(0, ahead_x), chosen(0, behind_x), chosen(1, g), chosen(2, g)]
    first = rhs - hop(weights, rhs, others, row)

    near_out[0] = first.astype(BF16)
    near_out[1] = (rhs - hop(weights, first, [], row)).astype(BF16)
    pushed = pushes(toward, first, row, lane)
    pairs = [(kx, kt) for kx in (0, 1) for kt in (2, 3)]
    for at, pair in enumerate(pairs):
        for side in range(2):
            skew_out[at, side] = pushed[pair[side]].astype(BF16)
    for k in range(4):
        far_out[k] = pushed[k].astype(BF16)

    def back(*ks):
        return device(-sum(ahead[k][0] for k in ks), -sum(ahead[k][1] for k in ks))

    mid_copies = (
        [
            remote(skew_out.at[at], mid_in.at[pl.ds(12 + 2 * at, 2)], mid_send, mid_recv, back(*pair))
            for at, pair in enumerate(pairs)
        ]
        + [
            remote(near_out, mid_in.at[pl.ds(2 * k, 2)], mid_send, mid_recv, back(k))
            for k in range(4)
        ]
        + [
            remote(far_out.at[k], mid_in.at[8 + k], mid_send, mid_recv, back(k, k))
            for k in range(4)
        ]
    )
    for copy in mid_copies:
        copy.start()
    arrived(mid_in, mid_recv)
    second = rhs - hop(weights, first, [mid_in[2 * k].astype(F32) for k in range(4)], row)
    around = []
    for k in range(4):
        value = mid_in[2 * k + 1].astype(F32) - mid_in[8 + k].astype(F32) - pushed[k ^ 1]
        for at, pair in enumerate(pairs):
            if k in pair:
                value = value - mid_in[12 + 2 * at + 1 - pair.index(k)].astype(F32)
        around.append(value)
    third = rhs - hop(weights, second, around, row)

    part = rhs - hop(weights, third, [], row)
    pushed = pushes(toward, third, row, lane)
    for at, piece in enumerate((part, pushed[0], pushed[1])):
        last_out[at] = piece.astype(BF16)
    keep_last = pltpu.make_async_copy(last_out, last_in.at[g], last_recv)
    keep_last.start()
    turn_out[0] = pushed[2].astype(BF16)
    turn_out[1] = pushed[3].astype(BF16)

    def last_copy(at, flip, i):
        src = last_out if at == 0 else turn_out.at[at - 1]
        dst = last_in.at[g] if at == 0 else turn_in.at[at - 1, g]
        return remote(
            src,
            dst,
            last_send if at == 0 else turn_send,
            last_recv if at == 0 else turn_recv,
            (member(flip, i), device(0, to_t[at])[1]),
        )

    for at, flip, count in broadcast:
        each(count, lambda i: last_copy(at, flip, i).start())
    block_here = jnp.int32(0)
    for k in range(n_group):
        block_here = block_here + jnp.where(g == k, owner[k], 0)
    arrived(last_in, last_recv)
    arrived(turn_in, turn_recv)

    def gathered(start, x):
        after, before = lax.rem(x + 1, n_group), lax.rem(x + n_group - 1, n_group)
        value = start
        for k in range(n_group):
            if start is None:
                mine = last_in[k, 0].astype(F32)
                mine = mine - turn_in[0, k].astype(F32) - turn_in[1, k].astype(F32)
                value = jnp.where(x == k, mine, 0.0) + (0.0 if value is None else value)
            else:
                mine = turn_in[0, k].astype(F32) + turn_in[1, k].astype(F32)
                value = value - jnp.where(x == k, mine, 0.0)
            value = value - jnp.where(after == k, last_in[k, 1].astype(F32), 0.0)
            value = value - jnp.where(before == k, last_in[k, 2].astype(F32), 0.0)
        return value

    sol_ref[...] = gathered(part, g)
    own_ref[...] = gathered(None, block_here).astype(BF16).astype(F32)

    arrived(rhs_in.at[pl.ds(0, 2)], rhs_send)
    arrived(rhs_in.at[2, pl.ds(0, n_group - 1)], rhs_send)
    arrived(link_in, link_send)
    arrived(mid_in, mid_send)
    arrived(last_in.at[pl.ds(0, n_group - 1)], last_send)
    arrived(turn_in, turn_send)


def on_device(n_group, n_sub, fine_residual, null_vectors, agg_map, block_owner, coarse_links):
    hbm = pl.BlockSpec(memory_space=pltpu.HBM)
    vmem = pl.BlockSpec(memory_space=pltpu.VMEM)
    dma = pltpu.SemaphoreType.DMA

    def piece(*lead):
        return pltpu.VMEM((*lead, 8, 128), BF16)

    in_hbm = functools.partial(pltpu.with_memory_space_constraint, memory_space=pltpu.HBM)
    solved = pl.pallas_call(
        functools.partial(kernel, n_group, n_sub),
        out_shape=(
            jax.ShapeDtypeStruct((8, 128), F32),
            jax.ShapeDtypeStruct((8, 128), F32),
            jax.ShapeDtypeStruct((NAGG, FS), F32),
            jax.ShapeDtypeStruct((2, SPIN_COLOR, NULLV, FS), BF16),
        ),
        in_specs=[hbm] * 5,
        out_specs=(vmem,) * 4,
        scratch_shapes=[
            pltpu.VMEM((2, SPIN_COLOR, RHS, FS), BF16),
            pltpu.VMEM((1, FS), jnp.int32),
            pltpu.VMEM((36, CDOF, CDOF), BF16),
            pltpu.SMEM((n_group,), jnp.int32),
            pltpu.VMEM((6 * 128, 256), BF16),
            pltpu.VMEM((128, 4 * 128), BF16),
            pltpu.VMEM((4, 128, 128), BF16),
            pltpu.VMEM((4, 128, 128), BF16),
            piece(),
            piece(3, n_group),
            piece(2),
            piece(4),
            piece(4, 2),
            piece(20),
            piece(3),
            piece(n_group, 3),
            piece(2),
            piece(2, n_group),
            dma((4 + NBLOCK,)),
        ]
        + [dma] * 10,
        compiler_params=pltpu.CompilerParams(
            collective_id=0, has_side_effects=True, vmem_limit_bytes=24 * 1024 * 1024
        ),
        name="coarse",
    )(
        in_hbm(block_owner),
        in_hbm(fine_residual),
        in_hbm(null_vectors),
        in_hbm(agg_map),
        in_hbm(coarse_links.reshape(36, CDOF, CDOF)),
    )
    solution_here, correction = pl.pallas_call(
        prolong_kernel,
        out_shape=(
            jax.ShapeDtypeStruct((2, 2, RHS, CDOF), F32),
            jax.ShapeDtypeStruct((2, SPIN_COLOR, RHS, FS), BF16),
        ),
        in_specs=[vmem] * 4,
        out_specs=(hbm, hbm),
        scratch_shapes=[
            pltpu.VMEM((2, 2, RHS, CDOF), F32),
            pltpu.VMEM((2, SPIN_COLOR, RHS, FS), BF16),
            dma((1 + NBLOCK,)),
        ],
        compiler_params=pltpu.CompilerParams(vmem_limit_bytes=24 * 1024 * 1024),
        name="prolong",
    )(*solved)
    return solution_here.reshape(1, 1, 2, 2, RHS, CDOF), correction


def solution(mesh):
    in_specs = (
        P(None, None, None, ("group", "sub")),
        P(None, None, None, ("group", "sub")),
        P(("group", "sub"), None),
        P(),
        P(None, "group", "sub", None, None, None, None),
    )
    out_specs = (P("group", "sub", None, None, None, None), P(None, None, None, ("group", "sub")))
    return jax.shard_map(
        functools.partial(on_device, mesh.shape["group"], mesh.shape["sub"]),
        mesh=mesh,
        in_specs=in_specs,
        out_specs=out_specs,
        check_vma=False,
    )
```

```python
import functools

import jax
import jax.numpy as jnp
from jax import lax
from jax.experimental import pallas as pl
from jax.experimental.pallas import tpu as pltpu
from jax.sharding import PartitionSpec as P

SPIN_COLOR = 12
NULLV = 32
AGG = 256
COARSE_STEPS = 4
RHS = 4
CDOF = 64
NAGG = 4
FS = NAGG * AGG
FBLOCK = 4
NBLOCK = SPIN_COLOR // FBLOCK
MESH = pl.DeviceIdType.MESH
F32 = jnp.float32
BF16 = jnp.bfloat16


def site_masks(agg_row):
    high = agg_row // 128
    low = agg_row % 128
    lanes = lax.broadcasted_iota(jnp.int32, (128, FS), 0)
    low_hot = jnp.where(lanes == low, 1.0, 0.0).astype(BF16)
    row = lax.broadcasted_iota(jnp.int32, (32, FS), 0)
    place = lax.broadcasted_iota(jnp.int32, (32, FS), 1)
    high_hot = jnp.where((row % 8 == high) & (row // 8 == place // AGG), 1.0, 0.0).astype(BF16)
    grid = lax.dot_general(
        high_hot, low_hot, (((1,), (1,)), ((), ())), preferred_element_type=F32
    )
    return [
        jnp.concatenate([grid[a * 8 + h : a * 8 + h + 1] for h in range(8)], axis=1)
        for a in range(NAGG)
    ]


def fold_lanes(tile):
    tile = tile + pltpu.roll(tile, 64, 1)
    return tile + pltpu.roll(tile, 32, 1)


def restricted_piece(total, row, lane):
    per_agg = []
    for a in range(NAGG):
        parts = []
        for ri in range(2):
            kept = jnp.zeros((8, 128), F32)
            for f in range(FBLOCK):
                at = (f * NAGG + a) * 8
                tile = total[at : at + 8, ri * 128 : (ri + 1) * 128]
                kept = kept + jnp.where(lane // NULLV == f, tile, 0.0)
            parts.append(fold_lanes(kept))
        by_re, by_im = parts
        real = by_re + pltpu.roll(by_im, 4, 0)
        imag = pltpu.roll(by_re, 4, 0) - by_im
        per_agg.append(jnp.where((lane // NULLV) % 2 == 0, real, imag))
    upper = jnp.where(lane < CDOF, per_agg[0], per_agg[1])
    lower = jnp.where(lane < CDOF, per_agg[2], per_agg[3])
    return jnp.where(row < 4, upper, pltpu.roll(lower, 4, 0))


def restrict(fine, null, masks, row, lane, loads=()):
    total = jnp.zeros((128, 256), F32)
    for b in range(NBLOCK):
        spread = []
        for f in range(b * FBLOCK, (b + 1) * FBLOCK):
            psi = jnp.concatenate([fine[0, f].astype(F32), fine[1, f].astype(F32)], axis=0)
            spread += [psi * masks[a] for a in range(NAGG)]
        spread = jnp.concatenate(spread, axis=0).astype(BF16)
        for load in loads[b : b + 1]:
            load.wait()
        part = null[:, b * FBLOCK : (b + 1) * FBLOCK].reshape(2 * FBLOCK * NULLV, FS)
        total = total + lax.dot_general(
            spread, part, (((1,), (1,)), ((), ())), preferred_element_type=F32
        )
    return restricted_piece(total, row, lane)


def prolongation_rows(piece, row, lane):
    block = lane // NULLV
    swapped = pltpu.roll(piece, 4, 0)
    doubled = (jnp.where(row < 4, piece, swapped), jnp.where(row < 4, swapped, piece))
    rows = []
    for y in range(2):
        for z in range(2):
            re, im = (
                fold_lanes(jnp.where(block == 2 * z + part, doubled[y], 0.0)) for part in range(2)
            )
            for left, right in ((re, -im), (im, re)):
                for pair in range(2):
                    same = block == 2 * pair + row // RHS
                    rows.append(
                        jnp.concatenate(
                            [jnp.where(same, left, 0.0), jnp.where(same, right, 0.0)], axis=1
                        )
                    )
    return jnp.concatenate(rows, axis=0).astype(BF16)


def prolong_kernel(sol_ref, own_ref, masks_ref, null, sol_out, corr_out, sol, corr, sem):
    row = lax.broadcasted_iota(jnp.int32, (8, 128), 0)
    lane = lax.broadcasted_iota(jnp.int32, (8, 128), 1)
    for y in range(2):
        for z in range(2):
            sol[y, z] = sol_ref[y * RHS : (y + 1) * RHS, z * CDOF : (z + 1) * CDOF]
    stores = [pltpu.make_async_copy(sol, sol_out, sem.at[NBLOCK])]
    stores[0].start()
    left = prolongation_rows(own_ref[...], row, lane)
    for b in range(NBLOCK):
        at_f = pl.ds(b * FBLOCK, FBLOCK)
        part = null[:, b * FBLOCK : (b + 1) * FBLOCK].reshape(2 * FBLOCK * NULLV, FS)
        wide = jnp.dot(left, part, preferred_element_type=F32)
        here = wide[:32] * masks_ref[0:1]
        for a in range(1, NAGG):
            here = here + wide[a * 32 : (a + 1) * 32] * masks_ref[a : a + 1]
        for ri in range(2):
            for f in range(FBLOCK):
                at = (ri * FBLOCK + f) * RHS
                corr[ri, b * FBLOCK + f] = here[at : at + RHS].astype(BF16)
        stores.append(
            pltpu.make_async_copy(corr.at[:, at_f], corr_out.at[:, at_f], sem.at[b])
        )
        stores[-1].start()
    for store in stores:
        store.wait()


def build_operator(links, weights):
    zero = jnp.zeros((CDOF, CDOF), BF16)

    def sited(block, z):
        return jnp.concatenate([block, zero] if z == 0 else [zero, block], axis=1)

    for y in range(2):
        for z in range(2):
            n = 2 * y + z
            here = links[0 * 4 + n]
            across = links[(7 + z) * 4 + n]
            columns = [
                jnp.concatenate([here, across] if z == 0 else [across, here], axis=1),
                sited(links[(5 + y) * 4 + n], z),
            ] + [sited(links[k * 4 + n], z) for k in (1, 2, 3, 4)]
            for source, column in enumerate(columns):
                weights[source * 128 : (source + 1) * 128, n * CDOF : (n + 1) * CDOF] = column.T


def hop(weights, pieces, start, row):
    low = jnp.concatenate(pieces, axis=1).astype(BF16)
    rows = weights[start * 128 : (start + len(pieces)) * 128]
    out = jnp.dot(low, rows, preferred_element_type=F32)
    return jnp.where(row < 4, out[:, :128], out[:, 128:])


def here_twice(here):
    return [here, pltpu.roll(here, 4, 0)]


def pushes(toward, here, row, lane):
    low = jnp.concatenate([jnp.where(lane < CDOF, here, 0.0), jnp.where(lane < CDOF, 0.0, here)], axis=0)
    out = jnp.dot(low.astype(BF16), toward[...], preferred_element_type=F32)
    parts = []
    for k in range(4):
        low_z, high_z = out[:8, k * 128 : (k + 1) * 128], out[8:, k * 128 : (k + 1) * 128]
        low_z = jnp.where(row < 4, low_z, pltpu.roll(low_z, CDOF, 1))
        high_z = jnp.where(row < 4, pltpu.roll(high_z, CDOF, 1), high_z)
        parts.append(jnp.where(lane < CDOF, low_z, high_z))
    return parts


def kernel(
    n_group,
    n_sub,
    owner_ref,
    fine_ref,
    null_ref,
    agg_ref,
    links_ref,
    sol_ref,
    own_ref,
    masks_ref,
    null,
    fine,
    agg,
    links,
    owner,
    weights,
    toward,
    link_out,
    rhs_out,
    rhs_in,
    near_out,
    near_in,
    far_out,
    skew_out,
    mid_in,
    last_out,
    last_in,
    turn_out,
    turn_in,
    local_sem,
    link_send,
    link_recv,
    rhs_send,
    rhs_recv,
    near_send,
    near_recv,
    mid_send,
    mid_recv,
    last_send,
    last_recv,
    turn_send,
    turn_recv,
):
    g = lax.axis_index("group")
    s = lax.axis_index("sub")
    half = n_group // 2
    chips = n_group // 4
    at_x, at_y, at_core = g // 4, (g // 2) % 2, g % 2

    def device(dg, ds):
        return lax.rem(g + (dg + n_group), n_group), lax.rem(s + (ds + n_sub), n_sub)

    def member(flip, i):
        x = lax.rem(at_x + (chips - 1 - i // 2), chips)
        return x * 4 + lax.rem(at_y + flip, 2) * 2 + lax.rem(at_core + 1 - i % 2, 2)

    def remote(src, dst, send, recv, to):
        return pltpu.make_async_remote_copy(
            src_ref=src, dst_ref=dst, send_sem=send, recv_sem=recv, device_id=to, device_id_type=MESH
        )

    def each(count, body):
        for i in range(count):
            body(i)

    def arrived(buffer, sem):
        pltpu.make_async_copy(buffer, buffer, sem).wait()

    load_agg = pltpu.make_async_copy(agg_ref, agg, local_sem.at[0])
    load_fine = pltpu.make_async_copy(fine_ref, fine, local_sem.at[1])
    load_links = pltpu.make_async_copy(links_ref, links, local_sem.at[2])
    load_null = [
        pltpu.make_async_copy(
            null_ref.at[:, pl.ds(b * FBLOCK, FBLOCK)],
            null.at[:, pl.ds(b * FBLOCK, FBLOCK)],
            local_sem.at[3 + b],
        )
        for b in range(NBLOCK)
    ]
    load_owner = pltpu.make_async_copy(owner_ref, owner, local_sem.at[3 + NBLOCK])
    to_t = (0, -1, 1)
    barrier = pltpu.get_barrier_semaphore()

    def greet(to):
        pl.semaphore_signal(barrier, inc=1, device_id=to, device_id_type=MESH)

    for flip in (1, 0):
        for at in (2, 1, 0):
            count = half - 1 if at == 0 and flip == 0 else half
            each(count, lambda i: greet((member(flip, i), device(0, to_t[at])[1])))
    greet(device(0, 2))
    greet(device(0, -2))

    load_agg.start()
    load_fine.start()
    for load in load_null:
        load.start()
    load_links.start()
    load_owner.start()

    row = lax.broadcasted_iota(jnp.int32, (8, 128), 0)
    lane = lax.broadcasted_iota(jnp.int32, (8, 128), 1)

    load_agg.wait()
    masks = site_masks(agg[...])
    for a in range(NAGG):
        masks_ref[a : a + 1] = masks[a]
    load_fine.wait()
    mine = restrict(fine, null, masks, row, lane, load_null).astype(BF16)
    rhs_out[...] = mine
    keep_rhs = pltpu.make_async_copy(rhs_out, rhs_in.at[0, g], rhs_recv.at[0])
    keep_rhs.start()

    ahead = ((1, 0), (-1, 0), (0, 1), (0, -1))
    load_links.wait()
    for k in range(4):
        at = (k + 1) * 4
        rows = [
            jnp.concatenate([links[at + 2 * y], links[at + 2 * y + 1]], axis=1) for y in range(2)
        ]
        link_out[k] = jnp.concatenate(rows, axis=0).T

    pl.semaphore_wait(barrier, 3 * n_group - 1 + 2)

    def rhs_copy(at, flip, i):
        return remote(
            rhs_out,
            rhs_in.at[at, g],
            rhs_send,
            rhs_recv.at[at],
            (member(flip, i), device(0, to_t[at])[1]),
        )

    broadcast = [
        (at, flip, half - 1 if at == 0 and flip == 0 else half) for flip in (1, 0) for at in (2, 1, 0)
    ]
    for at, flip, count in broadcast:
        each(count, lambda i: rhs_copy(at, flip, i).start())

    for k in range(4):
        remote(
            link_out.at[k],
            toward.at[:, pl.ds(k * 128, 128)],
            link_send,
            link_recv,
            device(*ahead[k]),
        ).start()
    build_operator(links, weights)
    load_owner.wait()

    def chosen(at, x):
        picked = jnp.zeros((8, 128), F32)
        for k in range(n_group):
            picked = picked + jnp.where(owner[k] == x, rhs_in[at, k].astype(F32), 0.0)
        return picked

    after, before = device(1, 0)[0], device(-1, 0)[0]
    arrived(rhs_in.at[0], rhs_recv.at[0])
    rhs = chosen(0, g)
    side = [chosen(0, after), chosen(0, before)]
    first = rhs - hop(weights, here_twice(rhs) + side, 0, row)
    for at in (1, 2):
        arrived(rhs_in.at[at], rhs_recv.at[at])
    first = first - hop(weights, [chosen(1, g), chosen(2, g)], 4, row)

    def back(*ks):
        return device(-sum(ahead[k][0] for k in ks), -sum(ahead[k][1] for k in ks))

    part = rhs - hop(weights, here_twice(first), 0, row)
    near_out[0] = first.astype(BF16)
    near_out[1] = part.astype(BF16)
    for k in range(4):
        remote(near_out, near_in.at[pl.ds(2 * k, 2)], near_send, near_recv, back(k)).start()
    arrived(toward, link_recv)
    pushed = pushes(toward, first, row, lane)
    pairs = [(kx, kt) for kx in (0, 1) for kt in (2, 3)]
    for at, pair in enumerate(pairs):
        for k in range(2):
            skew_out[at, k] = pushed[pair[k]].astype(BF16)
        remote(skew_out.at[at], mid_in.at[pl.ds(4 + 2 * at, 2)], mid_send, mid_recv, back(*pair)).start()
    for k in range(4):
        far_out[k] = pushed[k].astype(BF16)
        remote(far_out.at[k], mid_in.at[k], mid_send, mid_recv, back(k, k)).start()

    arrived(near_in, near_recv)
    second = part - hop(weights, [near_in[2 * k].astype(F32) for k in range(4)], 2, row)
    third = rhs - hop(weights, here_twice(second), 0, row)
    known = [near_in[2 * k + 1].astype(F32) - pushed[k ^ 1] for k in range(4)]
    arrived(mid_in, mid_recv)
    around = []
    for k in range(4):
        value = known[k] - mid_in[k].astype(F32)
        for at, pair in enumerate(pairs):
            if k in pair:
                value = value - mid_in[4 + 2 * at + 1 - pair.index(k)].astype(F32)
        around.append(value)
    third = third - hop(weights, around, 2, row)

    part = rhs - hop(weights, here_twice(third), 0, row)
    pushed = pushes(toward, third, row, lane)

    def wanted(at, place):
        block = owner[place]
        if at:
            return jnp.where(block == g, pushed[1 + at], 0.0)
        piece = jnp.where(block == g, part, 0.0)
        return piece - jnp.where(block == before, pushed[0], jnp.where(block == after, pushed[1], 0.0))

    for at, flip, count in broadcast:
        for i in range(count):
            place = member(flip, i)
            slot = at * n_group + flip * half + i
            last_out[slot] = wanted(at, place).astype(BF16)
            remote(
                last_out.at[slot],
                last_in.at[at * n_group + g],
                last_send,
                last_recv,
                (place, device(0, to_t[at])[1]),
            ).start()
    for k in range(4):
        turn_out[k] = pushed[k].astype(BF16)
        remote(turn_out.at[k], turn_in.at[k], turn_send, turn_recv, back(k)).start()
    kept = wanted(0, g).astype(BF16)
    last_out[half - 1] = kept
    keep_last = pltpu.make_async_copy(last_out.at[half - 1], last_in.at[g], last_recv)
    keep_last.start()

    arrived(turn_in, turn_recv)
    whole = part
    for k in range(4):
        whole = whole - turn_in[k].astype(F32)
    sol_ref[...] = whole
    arrived(last_in, last_recv)
    own = last_in[0].astype(F32)
    for k in range(1, n_group):
        own = own + last_in[k].astype(F32)
    turned = last_in[n_group].astype(F32)
    for k in range(n_group + 1, 3 * n_group):
        turned = turned + last_in[k].astype(F32)
    own_ref[...] = (own - turned).astype(BF16).astype(F32)

    arrived(rhs_in.at[pl.ds(0, 2)], rhs_send)
    arrived(rhs_in.at[2, pl.ds(0, n_group - 1)], rhs_send)
    arrived(toward, link_send)
    arrived(near_in, near_send)
    arrived(mid_in, mid_send)
    arrived(last_in.at[pl.ds(0, 3 * n_group - 1)], last_send)
    arrived(turn_in, turn_send)


def on_device(n_group, n_sub, fine_residual, null_vectors, agg_map, block_owner, coarse_links):
    hbm = pl.BlockSpec(memory_space=pltpu.HBM)
    vmem = pl.BlockSpec(memory_space=pltpu.VMEM)
    dma = pltpu.SemaphoreType.DMA

    def piece(*lead):
        return pltpu.VMEM((*lead, 8, 128), BF16)

    in_hbm = functools.partial(pltpu.with_memory_space_constraint, memory_space=pltpu.HBM)
    solved = pl.pallas_call(
        functools.partial(kernel, n_group, n_sub),
        out_shape=(
            jax.ShapeDtypeStruct((8, 128), F32),
            jax.ShapeDtypeStruct((8, 128), F32),
            jax.ShapeDtypeStruct((NAGG, FS), F32),
            jax.ShapeDtypeStruct((2, SPIN_COLOR, NULLV, FS), BF16),
        ),
        in_specs=[hbm] * 5,
        out_specs=(vmem,) * 4,
        scratch_shapes=[
            pltpu.VMEM((2, SPIN_COLOR, RHS, FS), BF16),
            pltpu.VMEM((1, FS), jnp.int32),
            pltpu.VMEM((36, CDOF, CDOF), BF16),
            pltpu.SMEM((n_group,), jnp.int32),
            pltpu.VMEM((6 * 128, 256), BF16),
            pltpu.VMEM((128, 4 * 128), BF16),
            pltpu.VMEM((4, 128, 128), BF16),
            piece(),
            piece(3, n_group),
            piece(2),
            piece(8),
            piece(4),
            piece(4, 2),
            piece(12),
            piece(3 * n_group),
            piece(3 * n_group),
            piece(4),
            piece(4),
            dma((4 + NBLOCK,)),
            dma,
            dma,
            dma,
            dma((3,)),
        ]
        + [dma] * 8,
        compiler_params=pltpu.CompilerParams(
            collective_id=0, has_side_effects=True, vmem_limit_bytes=24 * 1024 * 1024
        ),
        name="coarse",
    )(
        in_hbm(block_owner),
        in_hbm(fine_residual),
        in_hbm(null_vectors),
        in_hbm(agg_map),
        in_hbm(coarse_links.reshape(36, CDOF, CDOF)),
    )
    solution_here, correction = pl.pallas_call(
        prolong_kernel,
        out_shape=(
            jax.ShapeDtypeStruct((2, 2, RHS, CDOF), F32),
            jax.ShapeDtypeStruct((2, SPIN_COLOR, RHS, FS), BF16),
        ),
        in_specs=[vmem] * 4,
        out_specs=(hbm, hbm),
        scratch_shapes=[
            pltpu.VMEM((2, 2, RHS, CDOF), F32),
            pltpu.VMEM((2, SPIN_COLOR, RHS, FS), BF16),
            dma((1 + NBLOCK,)),
        ],
        compiler_params=pltpu.CompilerParams(vmem_limit_bytes=24 * 1024 * 1024),
        name="prolong",
    )(*solved)
    return solution_here.reshape(1, 1, 2, 2, RHS, CDOF), correction


def solution(mesh):
    in_specs = (
        P(None, None, None, ("group", "sub")),
        P(None, None, None, ("group", "sub")),
        P(("group", "sub"), None),
        P(),
        P(None, "group", "sub", None, None, None, None),
    )
    out_specs = (P("group", "sub", None, None, None, None), P(None, None, None, ("group", "sub")))
    return jax.shard_map(
        functools.partial(on_device, mesh.shape["group"], mesh.shape["sub"]),
        mesh=mesh,
        in_specs=in_specs,
        out_specs=out_specs,
        check_vma=False,
    )
```

```python
import functools

import jax
import jax.numpy as jnp
from jax import lax
from jax.experimental import pallas as pl
from jax.experimental.pallas import tpu as pltpu
from jax.sharding import PartitionSpec as P

SPIN_COLOR = 12
NULLV = 32
AGG = 256
COARSE_STEPS = 4
RHS = 4
CDOF = 64
NAGG = 4
FS = NAGG * AGG
FBLOCK = 4
NBLOCK = SPIN_COLOR // FBLOCK
MESH = pl.DeviceIdType.MESH
F32 = jnp.float32
BF16 = jnp.bfloat16


def site_masks(agg_row):
    high = agg_row // 128
    low = agg_row % 128
    lanes = lax.broadcasted_iota(jnp.int32, (128, FS), 0)
    low_hot = jnp.where(lanes == low, 1.0, 0.0).astype(BF16)
    row = lax.broadcasted_iota(jnp.int32, (32, FS), 0)
    place = lax.broadcasted_iota(jnp.int32, (32, FS), 1)
    high_hot = jnp.where((row % 8 == high) & (row // 8 == place // AGG), 1.0, 0.0).astype(BF16)
    grid = lax.dot_general(
        high_hot, low_hot, (((1,), (1,)), ((), ())), preferred_element_type=F32
    )
    return [
        jnp.concatenate([grid[a * 8 + h : a * 8 + h + 1] for h in range(8)], axis=1)
        for a in range(NAGG)
    ]


def fold_lanes(tile):
    tile = tile + pltpu.roll(tile, 64, 1)
    return tile + pltpu.roll(tile, 32, 1)


def restricted_piece(total, row, lane):
    per_agg = []
    for a in range(NAGG):
        parts = []
        for ri in range(2):
            kept = jnp.zeros((8, 128), F32)
            for f in range(FBLOCK):
                at = (f * NAGG + a) * 8
                tile = total[at : at + 8, ri * 128 : (ri + 1) * 128]
                kept = kept + jnp.where(lane // NULLV == f, tile, 0.0)
            parts.append(fold_lanes(kept))
        by_re, by_im = parts
        real = by_re + pltpu.roll(by_im, 4, 0)
        imag = pltpu.roll(by_re, 4, 0) - by_im
        per_agg.append(jnp.where((lane // NULLV) % 2 == 0, real, imag))
    upper = jnp.where(lane < CDOF, per_agg[0], per_agg[1])
    lower = jnp.where(lane < CDOF, per_agg[2], per_agg[3])
    return jnp.where(row < 4, upper, pltpu.roll(lower, 4, 0))


def restrict(fine, null, masks, row, lane, loads=()):
    total = jnp.zeros((128, 256), F32)
    for b in range(NBLOCK):
        spread = []
        for f in range(b * FBLOCK, (b + 1) * FBLOCK):
            psi = jnp.concatenate([fine[0, f].astype(F32), fine[1, f].astype(F32)], axis=0)
            spread += [psi * masks[a] for a in range(NAGG)]
        spread = jnp.concatenate(spread, axis=0).astype(BF16)
        for load in loads[b : b + 1]:
            load.wait()
        part = null[:, b * FBLOCK : (b + 1) * FBLOCK].reshape(2 * FBLOCK * NULLV, FS)
        total = total + lax.dot_general(
            spread, part, (((1,), (1,)), ((), ())), preferred_element_type=F32
        )
    return restricted_piece(total, row, lane)


def prolongation_rows(piece, row, lane):
    block = lane // NULLV
    swapped = pltpu.roll(piece, 4, 0)
    doubled = (jnp.where(row < 4, piece, swapped), jnp.where(row < 4, swapped, piece))
    rows = []
    for y in range(2):
        for z in range(2):
            re, im = (
                fold_lanes(jnp.where(block == 2 * z + part, doubled[y], 0.0)) for part in range(2)
            )
            for left, right in ((re, -im), (im, re)):
                for pair in range(2):
                    same = block == 2 * pair + row // RHS
                    rows.append(
                        jnp.concatenate(
                            [jnp.where(same, left, 0.0), jnp.where(same, right, 0.0)], axis=1
                        )
                    )
    return jnp.concatenate(rows, axis=0).astype(BF16)


def prolong_kernel(sol_ref, own_ref, masks_ref, null, sol_out, corr_out, sol, corr, sem):
    row = lax.broadcasted_iota(jnp.int32, (8, 128), 0)
    lane = lax.broadcasted_iota(jnp.int32, (8, 128), 1)
    for y in range(2):
        for z in range(2):
            sol[y, z] = sol_ref[y * RHS : (y + 1) * RHS, z * CDOF : (z + 1) * CDOF]
    stores = [pltpu.make_async_copy(sol, sol_out, sem.at[NBLOCK])]
    stores[0].start()
    inside = [
        jnp.broadcast_to(masks_ref[a : a + 1], (32, FS)) > 0.5 for a in range(1, NAGG)
    ]
    left = prolongation_rows(own_ref[...], row, lane)
    for b in range(NBLOCK):
        at_f = pl.ds(b * FBLOCK, FBLOCK)
        part = null[:, b * FBLOCK : (b + 1) * FBLOCK].reshape(2 * FBLOCK * NULLV, FS)
        wide = jnp.dot(left, part, preferred_element_type=F32)
        here = wide[:32]
        for a in range(1, NAGG):
            here = jnp.where(inside[a - 1], wide[a * 32 : (a + 1) * 32], here)
        for ri in range(2):
            for f in range(FBLOCK):
                at = (ri * FBLOCK + f) * RHS
                corr[ri, b * FBLOCK + f] = here[at : at + RHS].astype(BF16)
        stores.append(
            pltpu.make_async_copy(corr.at[:, at_f], corr_out.at[:, at_f], sem.at[b])
        )
        stores[-1].start()
    for store in stores:
        store.wait()


def build_operator(links, weights):
    zero = jnp.zeros((CDOF, CDOF), BF16)

    def sited(block, z):
        return jnp.concatenate([block, zero] if z == 0 else [zero, block], axis=1)

    for y in range(2):
        for z in range(2):
            n = 2 * y + z
            here = links[0 * 4 + n]
            across = links[(7 + z) * 4 + n]
            columns = [
                jnp.concatenate([here, across] if z == 0 else [across, here], axis=1),
                sited(links[(5 + y) * 4 + n], z),
            ] + [sited(links[k * 4 + n], z) for k in (1, 2, 3, 4)]
            for source, column in enumerate(columns):
                weights[source * 128 : (source + 1) * 128, n * CDOF : (n + 1) * CDOF] = column.T


def hop(weights, pieces, start, row):
    low = jnp.concatenate(pieces, axis=1).astype(BF16)
    rows = weights[start * 128 : (start + len(pieces)) * 128]
    out = jnp.dot(low, rows, preferred_element_type=F32)
    return jnp.where(row < 4, out[:, :128], out[:, 128:])


def here_twice(here):
    return [here, pltpu.roll(here, 4, 0)]


def pushes(toward, here, row, lane):
    low = jnp.concatenate([jnp.where(lane < CDOF, here, 0.0), jnp.where(lane < CDOF, 0.0, here)], axis=0)
    out = jnp.dot(low.astype(BF16), toward[...], preferred_element_type=F32)
    parts = []
    for k in range(4):
        low_z, high_z = out[:8, k * 128 : (k + 1) * 128], out[8:, k * 128 : (k + 1) * 128]
        low_z = jnp.where(row < 4, low_z, pltpu.roll(low_z, CDOF, 1))
        high_z = jnp.where(row < 4, pltpu.roll(high_z, CDOF, 1), high_z)
        parts.append(jnp.where(lane < CDOF, low_z, high_z))
    return parts


def kernel(
    n_group,
    n_sub,
    owner_ref,
    fine_ref,
    null_ref,
    agg_ref,
    links_ref,
    sol_ref,
    own_ref,
    masks_ref,
    null,
    fine,
    agg,
    links,
    owner,
    weights,
    toward,
    link_out,
    rhs_out,
    rhs_in,
    near_out,
    near_in,
    far_out,
    skew_out,
    mid_in,
    last_out,
    last_in,
    turn_out,
    turn_in,
    local_sem,
    link_send,
    link_recv,
    rhs_send,
    rhs_recv,
    near_send,
    near_recv,
    mid_send,
    mid_recv,
    last_send,
    last_recv,
    turn_send,
    turn_recv,
):
    g = lax.axis_index("group")
    s = lax.axis_index("sub")
    half = n_group // 2
    chips = n_group // 4
    at_x, at_y, at_core = g // 4, (g // 2) % 2, g % 2

    def device(dg, ds):
        return lax.rem(g + (dg + n_group), n_group), lax.rem(s + (ds + n_sub), n_sub)

    def member(flip, i):
        x = lax.rem(at_x + (chips - 1 - i // 2), chips)
        return x * 4 + lax.rem(at_y + flip, 2) * 2 + lax.rem(at_core + 1 - i % 2, 2)

    def remote(src, dst, send, recv, to):
        return pltpu.make_async_remote_copy(
            src_ref=src, dst_ref=dst, send_sem=send, recv_sem=recv, device_id=to, device_id_type=MESH
        )

    def each(count, body):
        for i in range(count):
            body(i)

    def arrived(buffer, sem):
        pltpu.make_async_copy(buffer, buffer, sem).wait()

    load_agg = pltpu.make_async_copy(agg_ref, agg, local_sem.at[0])
    load_fine = pltpu.make_async_copy(fine_ref, fine, local_sem.at[1])
    load_links = pltpu.make_async_copy(links_ref, links, local_sem.at[2])
    load_null = [
        pltpu.make_async_copy(
            null_ref.at[:, pl.ds(b * FBLOCK, FBLOCK)],
            null.at[:, pl.ds(b * FBLOCK, FBLOCK)],
            local_sem.at[3 + b],
        )
        for b in range(NBLOCK)
    ]
    load_owner = pltpu.make_async_copy(owner_ref, owner, local_sem.at[3 + NBLOCK])
    to_t = (0, -1, 1)
    barrier = pltpu.get_barrier_semaphore()

    def greet(to):
        pl.semaphore_signal(barrier, inc=1, device_id=to, device_id_type=MESH)

    for flip in (1, 0):
        for at in (2, 1, 0):
            count = half - 1 if at == 0 and flip == 0 else half
            each(count, lambda i: greet((member(flip, i), device(0, to_t[at])[1])))
    greet(device(0, 2))
    greet(device(0, -2))

    load_agg.start()
    load_fine.start()
    for load in load_null:
        load.start()
    load_links.start()
    load_owner.start()

    row = lax.broadcasted_iota(jnp.int32, (8, 128), 0)
    lane = lax.broadcasted_iota(jnp.int32, (8, 128), 1)

    load_agg.wait()
    masks = site_masks(agg[...])
    for a in range(NAGG):
        masks_ref[a : a + 1] = masks[a]
    load_fine.wait()
    mine = restrict(fine, null, masks, row, lane, load_null).astype(BF16)
    rhs_out[...] = mine
    keep_rhs = pltpu.make_async_copy(rhs_out, rhs_in.at[0, g], rhs_recv.at[0])
    keep_rhs.start()

    ahead = ((1, 0), (-1, 0), (0, 1), (0, -1))
    load_links.wait()
    for k in range(4):
        at = (k + 1) * 4
        rows = [
            jnp.concatenate([links[at + 2 * y], links[at + 2 * y + 1]], axis=1) for y in range(2)
        ]
        link_out[k] = jnp.concatenate(rows, axis=0).T

    pl.semaphore_wait(barrier, 3 * n_group - 1 + 2)

    def rhs_copy(at, flip, i):
        return remote(
            rhs_out,
            rhs_in.at[at, g],
            rhs_send,
            rhs_recv.at[at],
            (member(flip, i), device(0, to_t[at])[1]),
        )

    broadcast = [
        (at, flip, half - 1 if at == 0 and flip == 0 else half) for flip in (1, 0) for at in (2, 1, 0)
    ]
    for at, flip, count in broadcast:
        each(count, lambda i: rhs_copy(at, flip, i).start())

    for k in range(4):
        remote(
            link_out.at[k],
            toward.at[:, pl.ds(k * 128, 128)],
            link_send,
            link_recv,
            device(*ahead[k]),
        ).start()
    build_operator(links, weights)
    load_owner.wait()

    def chosen(at, x):
        picked = jnp.zeros((8, 128), F32)
        for k in range(n_group):
            picked = picked + jnp.where(owner[k] == x, rhs_in[at, k].astype(F32), 0.0)
        return picked

    after, before = device(1, 0)[0], device(-1, 0)[0]
    arrived(rhs_in.at[0], rhs_recv.at[0])
    rhs = chosen(0, g)
    side = [chosen(0, after), chosen(0, before)]
    first = rhs - hop(weights, here_twice(rhs) + side, 0, row)
    for at in (1, 2):
        arrived(rhs_in.at[at], rhs_recv.at[at])
    first = first - hop(weights, [chosen(1, g), chosen(2, g)], 4, row)

    def back(*ks):
        return device(-sum(ahead[k][0] for k in ks), -sum(ahead[k][1] for k in ks))

    arrived(toward, link_recv)
    pushed = pushes(toward, first, row, lane)
    pairs = [(kx, kt) for kx in (0, 1) for kt in (2, 3)]
    for at, pair in enumerate(pairs):
        for k in range(2):
            skew_out[at, k] = pushed[pair[k]].astype(BF16)
        remote(skew_out.at[at], mid_in.at[pl.ds(4 + 2 * at, 2)], mid_send, mid_recv, back(*pair)).start()
    for k in range(4):
        far_out[k] = pushed[k].astype(BF16)
        remote(far_out.at[k], mid_in.at[k], mid_send, mid_recv, back(k, k)).start()

    part = rhs - hop(weights, here_twice(first), 0, row)
    near_out[0] = first.astype(BF16)
    near_out[1] = part.astype(BF16)
    for k in range(4):
        remote(near_out, near_in.at[pl.ds(2 * k, 2)], near_send, near_recv, back(k)).start()

    arrived(near_in, near_recv)
    second = part - hop(weights, [near_in[2 * k].astype(F32) for k in range(4)], 2, row)
    third = rhs - hop(weights, here_twice(second), 0, row)
    known = [near_in[2 * k + 1].astype(F32) - pushed[k ^ 1] for k in range(4)]
    arrived(mid_in, mid_recv)
    around = []
    for k in range(4):
        value = known[k] - mid_in[k].astype(F32)
        for at, pair in enumerate(pairs):
            if k in pair:
                value = value - mid_in[4 + 2 * at + 1 - pair.index(k)].astype(F32)
        around.append(value)
    third = third - hop(weights, around, 2, row)

    part = rhs - hop(weights, here_twice(third), 0, row)
    pushed = pushes(toward, third, row, lane)

    def wanted(at, place):
        block = owner[place]
        if at:
            return jnp.where(block == g, pushed[1 + at], 0.0)
        piece = jnp.where(block == g, part, 0.0)
        return piece - jnp.where(block == before, pushed[0], jnp.where(block == after, pushed[1], 0.0))

    for at, flip, count in broadcast:
        for i in range(count):
            place = member(flip, i)
            slot = at * n_group + flip * half + i
            last_out[slot] = wanted(at, place).astype(BF16)
            remote(
                last_out.at[slot],
                last_in.at[at * n_group + g],
                last_send,
                last_recv.at[at],
                (place, device(0, to_t[at])[1]),
            ).start()
    for k in range(4):
        turn_out[k] = pushed[k].astype(BF16)
        remote(turn_out.at[k], turn_in.at[k], turn_send, turn_recv, back(k)).start()
    kept = wanted(0, g).astype(BF16)
    last_out[half - 1] = kept
    keep_last = pltpu.make_async_copy(last_out.at[half - 1], last_in.at[g], last_recv.at[0])
    keep_last.start()

    arrived(turn_in, turn_recv)
    whole = part
    for k in range(4):
        whole = whole - turn_in[k].astype(F32)
    sol_ref[...] = whole
    sums = []
    for at in range(3):
        arrived(last_in.at[pl.ds(at * n_group, n_group)], last_recv.at[at])
        parts = [last_in[at * n_group + k].astype(F32) for k in range(n_group)]
        while len(parts) > 1:
            parts = [parts[i] + parts[i + 1] for i in range(0, len(parts), 2)]
        sums.append(parts[0])
    own_ref[...] = (sums[0] - sums[1] - sums[2]).astype(BF16).astype(F32)

    arrived(rhs_in.at[pl.ds(0, 2)], rhs_send)
    arrived(rhs_in.at[2, pl.ds(0, n_group - 1)], rhs_send)
    arrived(toward, link_send)
    arrived(near_in, near_send)
    arrived(mid_in, mid_send)
    arrived(last_in.at[pl.ds(0, 3 * n_group - 1)], last_send)
    arrived(turn_in, turn_send)


def on_device(n_group, n_sub, fine_residual, null_vectors, agg_map, block_owner, coarse_links):
    hbm = pl.BlockSpec(memory_space=pltpu.HBM)
    vmem = pl.BlockSpec(memory_space=pltpu.VMEM)
    dma = pltpu.SemaphoreType.DMA

    def piece(*lead):
        return pltpu.VMEM((*lead, 8, 128), BF16)

    in_hbm = functools.partial(pltpu.with_memory_space_constraint, memory_space=pltpu.HBM)
    solved = pl.pallas_call(
        functools.partial(kernel, n_group, n_sub),
        out_shape=(
            jax.ShapeDtypeStruct((8, 128), F32),
            jax.ShapeDtypeStruct((8, 128), F32),
            jax.ShapeDtypeStruct((NAGG, FS), F32),
            jax.ShapeDtypeStruct((2, SPIN_COLOR, NULLV, FS), BF16),
        ),
        in_specs=[hbm] * 5,
        out_specs=(vmem,) * 4,
        scratch_shapes=[
            pltpu.VMEM((2, SPIN_COLOR, RHS, FS), BF16),
            pltpu.VMEM((1, FS), jnp.int32),
            pltpu.VMEM((36, CDOF, CDOF), BF16),
            pltpu.SMEM((n_group,), jnp.int32),
            pltpu.VMEM((6 * 128, 256), BF16),
            pltpu.VMEM((128, 4 * 128), BF16),
            pltpu.VMEM((4, 128, 128), BF16),
            piece(),
            piece(3, n_group),
            piece(2),
            piece(8),
            piece(4),
            piece(4, 2),
            piece(12),
            piece(3 * n_group),
            piece(3 * n_group),
            piece(4),
            piece(4),
            dma((4 + NBLOCK,)),
            dma,
            dma,
            dma,
            dma((3,)),
        ]
        + [dma] * 5
        + [dma((3,)), dma, dma],
        compiler_params=pltpu.CompilerParams(
            collective_id=0, has_side_effects=True, vmem_limit_bytes=24 * 1024 * 1024
        ),
        name="coarse",
    )(
        in_hbm(block_owner),
        in_hbm(fine_residual),
        in_hbm(null_vectors),
        in_hbm(agg_map),
        in_hbm(coarse_links.reshape(36, CDOF, CDOF)),
    )
    solution_here, correction = pl.pallas_call(
        prolong_kernel,
        out_shape=(
            jax.ShapeDtypeStruct((2, 2, RHS, CDOF), F32),
            jax.ShapeDtypeStruct((2, SPIN_COLOR, RHS, FS), BF16),
        ),
        in_specs=[vmem] * 4,
        out_specs=(hbm, hbm),
        scratch_shapes=[
            pltpu.VMEM((2, 2, RHS, CDOF), F32),
            pltpu.VMEM((2, SPIN_COLOR, RHS, FS), BF16),
            dma((1 + NBLOCK,)),
        ],
        compiler_params=pltpu.CompilerParams(vmem_limit_bytes=24 * 1024 * 1024),
        name="prolong",
    )(*solved)
    return solution_here.reshape(1, 1, 2, 2, RHS, CDOF), correction


def solution(mesh):
    in_specs = (
        P(None, None, None, ("group", "sub")),
        P(None, None, None, ("group", "sub")),
        P(("group", "sub"), None),
        P(),
        P(None, "group", "sub", None, None, None, None),
    )
    out_specs = (P("group", "sub", None, None, None, None), P(None, None, None, ("group", "sub")))
    return jax.shard_map(
        functools.partial(on_device, mesh.shape["group"], mesh.shape["sub"]),
        mesh=mesh,
        in_specs=in_specs,
        out_specs=out_specs,
        check_vma=False,
    )
```

```python
import functools

import jax
import jax.numpy as jnp
from jax import lax
from jax.experimental import pallas as pl
from jax.experimental.pallas import tpu as pltpu
from jax.sharding import PartitionSpec as P

SPIN_COLOR = 12
NULLV = 32
AGG = 256
COARSE_STEPS = 4
RHS = 4
CDOF = 64
NAGG = 4
FS = NAGG * AGG
FBLOCK = 4
NBLOCK = SPIN_COLOR // FBLOCK
MESH = pl.DeviceIdType.MESH
F32 = jnp.float32
BF16 = jnp.bfloat16


def site_masks(agg_row):
    high = agg_row // 128
    low = agg_row % 128
    lanes = lax.broadcasted_iota(jnp.int32, (128, FS), 0)
    low_hot = jnp.where(lanes == low, 1.0, 0.0).astype(BF16)
    row = lax.broadcasted_iota(jnp.int32, (32, FS), 0)
    place = lax.broadcasted_iota(jnp.int32, (32, FS), 1)
    high_hot = jnp.where((row % 8 == high) & (row // 8 == place // AGG), 1.0, 0.0).astype(BF16)
    grid = lax.dot_general(
        high_hot, low_hot, (((1,), (1,)), ((), ())), preferred_element_type=F32
    )
    return [
        jnp.concatenate([grid[a * 8 + h : a * 8 + h + 1] for h in range(8)], axis=1)
        for a in range(NAGG)
    ]


def fold_lanes(tile):
    tile = tile + pltpu.roll(tile, 64, 1)
    return tile + pltpu.roll(tile, 32, 1)


def restricted_piece(total, row, lane):
    per_agg = []
    for a in range(NAGG):
        parts = []
        for ri in range(2):
            kept = jnp.zeros((8, 128), F32)
            for f in range(FBLOCK):
                at = (f * NAGG + a) * 8
                tile = total[at : at + 8, ri * 128 : (ri + 1) * 128]
                kept = kept + jnp.where(lane // NULLV == f, tile, 0.0)
            parts.append(fold_lanes(kept))
        by_re, by_im = parts
        real = by_re + pltpu.roll(by_im, 4, 0)
        imag = pltpu.roll(by_re, 4, 0) - by_im
        per_agg.append(jnp.where((lane // NULLV) % 2 == 0, real, imag))
    upper = jnp.where(lane < CDOF, per_agg[0], per_agg[1])
    lower = jnp.where(lane < CDOF, per_agg[2], per_agg[3])
    return jnp.where(row < 4, upper, pltpu.roll(lower, 4, 0))


def restrict(fine, null, masks, row, lane, loads=()):
    total = jnp.zeros((128, 256), F32)
    for b in range(NBLOCK):
        spread = []
        for f in range(b * FBLOCK, (b + 1) * FBLOCK):
            psi = jnp.concatenate([fine[0, f].astype(F32), fine[1, f].astype(F32)], axis=0)
            spread += [psi * masks[a] for a in range(NAGG)]
        spread = jnp.concatenate(spread, axis=0).astype(BF16)
        for load in loads[b : b + 1]:
            load.wait()
        part = null[:, b * FBLOCK : (b + 1) * FBLOCK].reshape(2 * FBLOCK * NULLV, FS)
        total = total + lax.dot_general(
            spread, part, (((1,), (1,)), ((), ())), preferred_element_type=F32
        )
    return restricted_piece(total, row, lane)


def prolongation_rows(piece, row, lane):
    block = lane // NULLV
    swapped = pltpu.roll(piece, 4, 0)
    doubled = (jnp.where(row < 4, piece, swapped), jnp.where(row < 4, swapped, piece))
    rows = []
    for y in range(2):
        for z in range(2):
            re, im = (
                fold_lanes(jnp.where(block == 2 * z + part, doubled[y], 0.0)) for part in range(2)
            )
            for left, right in ((re, -im), (im, re)):
                for pair in range(2):
                    same = block == 2 * pair + row // RHS
                    rows.append(
                        jnp.concatenate(
                            [jnp.where(same, left, 0.0), jnp.where(same, right, 0.0)], axis=1
                        )
                    )
    return jnp.concatenate(rows, axis=0).astype(BF16)


def prolong_kernel(sol_ref, own_ref, masks_ref, null, sol_out, corr_out, sol, corr, sem):
    row = lax.broadcasted_iota(jnp.int32, (8, 128), 0)
    lane = lax.broadcasted_iota(jnp.int32, (8, 128), 1)
    for y in range(2):
        for z in range(2):
            sol[y, z] = sol_ref[y * RHS : (y + 1) * RHS, z * CDOF : (z + 1) * CDOF]
    stores = [pltpu.make_async_copy(sol, sol_out, sem.at[NBLOCK])]
    stores[0].start()
    left = prolongation_rows(own_ref[...], row, lane)
    for b in range(NBLOCK):
        at_f = pl.ds(b * FBLOCK, FBLOCK)
        part = null[:, b * FBLOCK : (b + 1) * FBLOCK].reshape(2 * FBLOCK * NULLV, FS)
        wide = jnp.dot(left, part, preferred_element_type=F32)
        here = wide[:32] * masks_ref[0:1]
        for a in range(1, NAGG):
            here = here + wide[a * 32 : (a + 1) * 32] * masks_ref[a : a + 1]
        for ri in range(2):
            for f in range(FBLOCK):
                at = (ri * FBLOCK + f) * RHS
                corr[ri, b * FBLOCK + f] = here[at : at + RHS].astype(BF16)
        stores.append(
            pltpu.make_async_copy(corr.at[:, at_f], corr_out.at[:, at_f], sem.at[b])
        )
        stores[-1].start()
    for store in stores:
        store.wait()


def build_operator(links, weights):
    zero = jnp.zeros((CDOF, CDOF), BF16)

    def sited(block, z):
        return jnp.concatenate([block, zero] if z == 0 else [zero, block], axis=1)

    for y in range(2):
        for z in range(2):
            n = 2 * y + z
            here = links[0 * 4 + n]
            across = links[(7 + z) * 4 + n]
            columns = [
                jnp.concatenate([here, across] if z == 0 else [across, here], axis=1),
                sited(links[(5 + y) * 4 + n], z),
            ] + [sited(links[k * 4 + n], z) for k in (1, 2, 3, 4)]
            for source, column in enumerate(columns):
                weights[source * 128 : (source + 1) * 128, n * CDOF : (n + 1) * CDOF] = column.T


def hop(weights, pieces, start, row):
    low = jnp.concatenate(pieces, axis=1).astype(BF16)
    rows = weights[start * 128 : (start + len(pieces)) * 128]
    out = jnp.dot(low, rows, preferred_element_type=F32)
    return jnp.where(row < 4, out[:, :128], out[:, 128:])


def here_twice(here):
    return [here, pltpu.roll(here, 4, 0)]


def pushes(toward, here, row, lane):
    low = jnp.concatenate([jnp.where(lane < CDOF, here, 0.0), jnp.where(lane < CDOF, 0.0, here)], axis=0)
    out = jnp.dot(low.astype(BF16), toward[...], preferred_element_type=F32)
    parts = []
    for k in range(4):
        low_z, high_z = out[:8, k * 128 : (k + 1) * 128], out[8:, k * 128 : (k + 1) * 128]
        low_z = jnp.where(row < 4, low_z, pltpu.roll(low_z, CDOF, 1))
        high_z = jnp.where(row < 4, pltpu.roll(high_z, CDOF, 1), high_z)
        parts.append(jnp.where(lane < CDOF, low_z, high_z))
    return parts


def kernel(
    n_group,
    n_sub,
    owner_ref,
    fine_ref,
    null_ref,
    agg_ref,
    links_ref,
    sol_ref,
    own_ref,
    masks_ref,
    null,
    fine,
    agg,
    links,
    owner,
    weights,
    toward,
    link_out,
    rhs_out,
    rhs_in,
    near_out,
    near_in,
    far_out,
    skew_out,
    mid_in,
    last_out,
    last_in,
    turn_out,
    turn_in,
    local_sem,
    link_send,
    link_recv,
    rhs_send,
    rhs_recv,
    near_send,
    near_recv,
    mid_send,
    mid_recv,
    last_send,
    last_recv,
    turn_send,
    turn_recv,
):
    g = lax.axis_index("group")
    s = lax.axis_index("sub")
    half = n_group // 2
    chips = n_group // 4
    at_x, at_y, at_core = g // 4, (g // 2) % 2, g % 2

    def device(dg, ds):
        return lax.rem(g + (dg + n_group), n_group), lax.rem(s + (ds + n_sub), n_sub)

    def member(flip, i):
        x = lax.rem(at_x + (chips - 1 - i // 2), chips)
        return x * 4 + lax.rem(at_y + flip, 2) * 2 + lax.rem(at_core + 1 - i % 2, 2)

    def remote(src, dst, send, recv, to):
        return pltpu.make_async_remote_copy(
            src_ref=src, dst_ref=dst, send_sem=send, recv_sem=recv, device_id=to, device_id_type=MESH
        )

    def each(count, body):
        for i in range(count):
            body(i)

    def arrived(buffer, sem):
        pltpu.make_async_copy(buffer, buffer, sem).wait()

    load_agg = pltpu.make_async_copy(agg_ref, agg, local_sem.at[0])
    load_fine = pltpu.make_async_copy(fine_ref, fine, local_sem.at[1])
    load_links = pltpu.make_async_copy(links_ref, links, local_sem.at[2])
    load_null = [
        pltpu.make_async_copy(
            null_ref.at[:, pl.ds(b * FBLOCK, FBLOCK)],
            null.at[:, pl.ds(b * FBLOCK, FBLOCK)],
            local_sem.at[3 + b],
        )
        for b in range(NBLOCK)
    ]
    load_owner = pltpu.make_async_copy(owner_ref, owner, local_sem.at[3 + NBLOCK])
    load_agg.start()
    load_fine.start()
    for load in load_null:
        load.start()
    load_links.start()
    load_owner.start()

    to_t = (0, -1, 1)
    barrier = pltpu.get_barrier_semaphore()

    def greet(to):
        pl.semaphore_signal(barrier, inc=1, device_id=to, device_id_type=MESH)

    for flip in (1, 0):
        for at in (2, 1, 0):
            count = half - 1 if at == 0 and flip == 0 else half
            each(count, lambda i: greet((member(flip, i), device(0, to_t[at])[1])))
    greet(device(0, 2))
    greet(device(0, -2))

    row = lax.broadcasted_iota(jnp.int32, (8, 128), 0)
    lane = lax.broadcasted_iota(jnp.int32, (8, 128), 1)

    load_agg.wait()
    masks = site_masks(agg[...])
    for a in range(NAGG):
        masks_ref[a : a + 1] = masks[a]
    load_fine.wait()
    mine = restrict(fine, null, masks, row, lane, load_null).astype(BF16)
    rhs_out[...] = mine
    keep_rhs = pltpu.make_async_copy(rhs_out, rhs_in.at[0, g], rhs_recv.at[0])
    keep_rhs.start()

    ahead = ((1, 0), (-1, 0), (0, 1), (0, -1))
    load_links.wait()
    for k in range(4):
        at = (k + 1) * 4
        rows = [
            jnp.concatenate([links[at + 2 * y], links[at + 2 * y + 1]], axis=1) for y in range(2)
        ]
        link_out[k] = jnp.concatenate(rows, axis=0).T

    pl.semaphore_wait(barrier, 3 * n_group - 1 + 2)

    def rhs_copy(at, flip, i):
        return remote(
            rhs_out,
            rhs_in.at[at, g],
            rhs_send,
            rhs_recv.at[at],
            (member(flip, i), device(0, to_t[at])[1]),
        )

    broadcast = [
        (at, flip, half - 1 if at == 0 and flip == 0 else half) for flip in (1, 0) for at in (2, 1, 0)
    ]
    for at, flip, count in broadcast:
        each(count, lambda i: rhs_copy(at, flip, i).start())

    for k in range(4):
        remote(
            link_out.at[k],
            toward.at[:, pl.ds(k * 128, 128)],
            link_send,
            link_recv,
            device(*ahead[k]),
        ).start()
    build_operator(links, weights)
    load_owner.wait()

    def chosen(at, x):
        picked = jnp.zeros((8, 128), F32)
        for k in range(n_group):
            picked = picked + jnp.where(owner[k] == x, rhs_in[at, k].astype(F32), 0.0)
        return picked

    after, before = device(1, 0)[0], device(-1, 0)[0]
    arrived(rhs_in.at[0], rhs_recv.at[0])
    rhs = chosen(0, g)
    side = [chosen(0, after), chosen(0, before)]
    first = rhs - hop(weights, here_twice(rhs) + side, 0, row)
    for at in (1, 2):
        arrived(rhs_in.at[at], rhs_recv.at[at])
    first = first - hop(weights, [chosen(1, g), chosen(2, g)], 4, row)

    def back(*ks):
        return device(-sum(ahead[k][0] for k in ks), -sum(ahead[k][1] for k in ks))

    part = rhs - hop(weights, here_twice(first), 0, row)
    near_out[0] = first.astype(BF16)
    near_out[1] = part.astype(BF16)
    for k in range(4):
        remote(near_out, near_in.at[pl.ds(2 * k, 2)], near_send, near_recv, back(k)).start()
    arrived(toward, link_recv)
    pushed = pushes(toward, first, row, lane)
    pairs = [(kx, kt) for kx in (0, 1) for kt in (2, 3)]
    for at, pair in enumerate(pairs):
        for k in range(2):
            skew_out[at, k] = pushed[pair[k]].astype(BF16)
        remote(skew_out.at[at], mid_in.at[pl.ds(4 + 2 * at, 2)], mid_send, mid_recv, back(*pair)).start()
    for k in range(4):
        far_out[k] = pushed[k].astype(BF16)
        remote(far_out.at[k], mid_in.at[k], mid_send, mid_recv, back(k, k)).start()

    arrived(near_in, near_recv)
    second = part - hop(weights, [near_in[2 * k].astype(F32) for k in range(4)], 2, row)
    third = rhs - hop(weights, here_twice(second), 0, row)
    known = [near_in[2 * k + 1].astype(F32) - pushed[k ^ 1] for k in range(4)]
    arrived(mid_in, mid_recv)
    around = []
    for k in range(4):
        value = known[k] - mid_in[k].astype(F32)
        for at, pair in enumerate(pairs):
            if k in pair:
                value = value - mid_in[4 + 2 * at + 1 - pair.index(k)].astype(F32)
        around.append(value)
    third = third - hop(weights, around, 2, row)

    part = rhs - hop(weights, here_twice(third), 0, row)
    pushed = pushes(toward, third, row, lane)

    def wanted(at, place):
        block = owner[place]
        if at:
            return jnp.where(block == g, pushed[1 + at], 0.0)
        piece = jnp.where(block == g, part, 0.0)
        return piece - jnp.where(block == before, pushed[0], jnp.where(block == after, pushed[1], 0.0))

    for at, flip, count in broadcast:
        for i in range(count):
            place = member(flip, i)
            slot = at * n_group + flip * half + i
            last_out[slot] = wanted(at, place).astype(BF16)
            remote(
                last_out.at[slot],
                last_in.at[at * n_group + g],
                last_send,
                last_recv,
                (place, device(0, to_t[at])[1]),
            ).start()
    for k in range(4):
        turn_out[k] = pushed[k].astype(BF16)
        remote(turn_out.at[k], turn_in.at[k], turn_send, turn_recv, back(k)).start()
    kept = wanted(0, g).astype(BF16)
    last_out[half - 1] = kept
    keep_last = pltpu.make_async_copy(last_out.at[half - 1], last_in.at[g], last_recv)
    keep_last.start()

    arrived(turn_in, turn_recv)
    whole = part
    for k in range(4):
        whole = whole - turn_in[k].astype(F32)
    sol_ref[...] = whole
    arrived(last_in, last_recv)
    own = last_in[0].astype(F32)
    for k in range(1, n_group):
        own = own + last_in[k].astype(F32)
    turned = last_in[n_group].astype(F32)
    for k in range(n_group + 1, 3 * n_group):
        turned = turned + last_in[k].astype(F32)
    own_ref[...] = (own - turned).astype(BF16).astype(F32)

    arrived(rhs_in.at[pl.ds(0, 2)], rhs_send)
    arrived(rhs_in.at[2, pl.ds(0, n_group - 1)], rhs_send)
    arrived(toward, link_send)
    arrived(near_in, near_send)
    arrived(mid_in, mid_send)
    arrived(last_in.at[pl.ds(0, 3 * n_group - 1)], last_send)
    arrived(turn_in, turn_send)


def on_device(n_group, n_sub, fine_residual, null_vectors, agg_map, block_owner, coarse_links):
    hbm = pl.BlockSpec(memory_space=pltpu.HBM)
    vmem = pl.BlockSpec(memory_space=pltpu.VMEM)
    dma = pltpu.SemaphoreType.DMA

    def piece(*lead):
        return pltpu.VMEM((*lead, 8, 128), BF16)

    in_hbm = functools.partial(pltpu.with_memory_space_constraint, memory_space=pltpu.HBM)
    solved = pl.pallas_call(
        functools.partial(kernel, n_group, n_sub),
        out_shape=(
            jax.ShapeDtypeStruct((8, 128), F32),
            jax.ShapeDtypeStruct((8, 128), F32),
            jax.ShapeDtypeStruct((NAGG, FS), F32),
            jax.ShapeDtypeStruct((2, SPIN_COLOR, NULLV, FS), BF16),
        ),
        in_specs=[hbm] * 5,
        out_specs=(vmem,) * 4,
        scratch_shapes=[
            pltpu.VMEM((2, SPIN_COLOR, RHS, FS), BF16),
            pltpu.VMEM((1, FS), jnp.int32),
            pltpu.VMEM((36, CDOF, CDOF), BF16),
            pltpu.SMEM((n_group,), jnp.int32),
            pltpu.VMEM((6 * 128, 256), BF16),
            pltpu.VMEM((128, 4 * 128), BF16),
            pltpu.VMEM((4, 128, 128), BF16),
            piece(),
            piece(3, n_group),
            piece(2),
            piece(8),
            piece(4),
            piece(4, 2),
            piece(12),
            piece(3 * n_group),
            piece(3 * n_group),
            piece(4),
            piece(4),
            dma((4 + NBLOCK,)),
            dma,
            dma,
            dma,
            dma((3,)),
        ]
        + [dma] * 8,
        compiler_params=pltpu.CompilerParams(
            collective_id=0, has_side_effects=True, vmem_limit_bytes=24 * 1024 * 1024
        ),
        name="coarse",
    )(
        in_hbm(block_owner),
        in_hbm(fine_residual),
        in_hbm(null_vectors),
        in_hbm(agg_map),
        in_hbm(coarse_links.reshape(36, CDOF, CDOF)),
    )
    solution_here, correction = pl.pallas_call(
        prolong_kernel,
        out_shape=(
            jax.ShapeDtypeStruct((2, 2, RHS, CDOF), F32),
            jax.ShapeDtypeStruct((2, SPIN_COLOR, RHS, FS), BF16),
        ),
        in_specs=[vmem] * 4,
        out_specs=(hbm, hbm),
        scratch_shapes=[
            pltpu.VMEM((2, 2, RHS, CDOF), F32),
            pltpu.VMEM((2, SPIN_COLOR, RHS, FS), BF16),
            dma((1 + NBLOCK,)),
        ],
        compiler_params=pltpu.CompilerParams(vmem_limit_bytes=24 * 1024 * 1024),
        name="prolong",
    )(*solved)
    return solution_here.reshape(1, 1, 2, 2, RHS, CDOF), correction


def solution(mesh):
    in_specs = (
        P(None, None, None, ("group", "sub")),
        P(None, None, None, ("group", "sub")),
        P(("group", "sub"), None),
        P(),
        P(None, "group", "sub", None, None, None, None),
    )
    out_specs = (P("group", "sub", None, None, None, None), P(None, None, None, ("group", "sub")))
    return jax.shard_map(
        functools.partial(on_device, mesh.shape["group"], mesh.shape["sub"]),
        mesh=mesh,
        in_specs=in_specs,
        out_specs=out_specs,
        check_vma=False,
    )
```
